256 devices in a mesh: rows: 64 (over y, z, core), dp: 4 (over x).
Axes of the slice: x: 4, y: 4, z: 8, core: 2. Of those that a mesh axis runs over, the one named last changes fastest.
Arguments:
- tokens: bfloat16 [4, 1024, 128, 256], P('dp', 'rows'), may hold values from -6 to 6
- norm_gain: float32 [256], replicated, may hold values from 0.1 to 1.9
- in_weight: bfloat16 [256, 768], replicated, may hold values from -16 to 16
- out_weight: bfloat16 [256, 256], replicated, may hold values from -0.375 to 0.375
- cotangent: bfloat16 [4, 1024, 128, 256], P('dp', 'rows'), may hold values from -6 to 6
Outputs:
- grad_tokens: bfloat16 [4, 1024, 128, 256], P('dp', 'rows')
- grad_in_weight: float32 [256, 768], replicated
- grad_out_weight: float32 [256, 256], replicated
- grad_gain: float32 [256], replicated
The draws below stay inside these ranges and needn't reach their ends.
All inputs are finite; a program needn't handle non-finite values.
Results may differ from the reference program's by a relative error of at most 0.011.
Values may be sent and summed in bfloat16 or wider, within the bound.
A program may use at most 128 MiB of HBM per device.

```python
import math
import jax
import jax.numpy as jnp
from jax import lax

D = 256
HEAD = 64
RADIUS = 3
COLS = 128
ROWS_ALL = 1024
BATCH = 4


def draw_in_weight(key, part):
    key = jax.random.fold_in(key, 7)
    base_key = jax.random.fold_in(key, 0)
    base = jnp.clip(jax.random.normal(base_key, (D, 3 * D), jnp.float32), -6.0, 6.0) * D ** (-0.5)
    return jnp.clip(base, -15.9, 15.9).astype(jnp.bfloat16)


def block_scale(own_key, shape, cuts, low, top_value):
    def one(dim, parts):
        heights = jax.random.uniform(jax.random.fold_in(jax.random.fold_in(own_key, 6), dim), (parts,), jnp.float32, low / len(cuts), top_value / len(cuts))
        return jnp.repeat(jnp.exp(heights), shape[dim] // parts).reshape((-1,) + (1,) * (len(shape) - dim - 1))

    level = one(*cuts[0])
    for cut in cuts[1:]:
        level = level * one(*cut)
    return level


def bell_draw(key, shape, deviation, limit, shards=(), held_as=jnp.bfloat16):
    loudness = block_scale(key, shape, shards, -0.22, 0.18) if shards else 1.0
    drawn = jax.random.normal(key, shape, jnp.float32) * deviation * loudness
    return jnp.minimum(jnp.maximum(drawn, -limit), limit).astype(held_as)


def setup_inputs(seed: int = 0) -> dict:
    key_of = jax.random.split(jax.random.key(seed), 6)
    return {
        "tokens": bell_draw(key_of[0], (BATCH, ROWS_ALL, COLS, D), 1.0, 6.0, ((0, 4), (1, 64))),
        "norm_gain": jnp.clip(1.0 + 0.18 * jax.random.normal(key_of[1], (D,), jnp.float32), 0.1, 1.9),
        "in_weight": draw_in_weight(jax.random.fold_in(key_of[5], 71), 0),
        "out_weight": bell_draw(key_of[3], (D, D), D ** -0.5, 0.375),
        "cotangent": bell_draw(key_of[4], (BATCH, ROWS_ALL, COLS, D), 1.0, 6.0, ((0, 4), (1, 64))),
    }


def one_image(image_pair, norm_gain, in_weight, out_weight):
    image, upstream = image_pair
    height, breadth, model_width = image.shape
    head_count = model_width // HEAD
    window = 2 * RADIUS + 1
    wide_input = image.astype(jnp.float32)
    inv_rms = lax.rsqrt(lax.optimization_barrier(jnp.mean(wide_input * wide_input, axis=-1, keepdims=True)) + 1e-06)
    normed = (wide_input * inv_rms * norm_gain).astype(jnp.bfloat16)
    flat_norm = normed.reshape(-1, model_width)
    projected = jnp.dot(flat_norm, in_weight, preferred_element_type=jnp.float32).astype(jnp.bfloat16)
    projected = lax.optimization_barrier(projected).astype(jnp.float32)
    projected = projected.reshape(height, breadth, 3, head_count, HEAD)
    padding = ((RADIUS, RADIUS), (RADIUS, RADIUS), (0, 0), (0, 0))
    queries = projected[:, :, 0]
    keys_pad = jnp.pad(projected[:, :, 1], padding)
    values_pad = jnp.pad(projected[:, :, 2], padding)
    row_ok = jnp.pad(jnp.ones((height,), jnp.float32), RADIUS)
    col_ok = jnp.pad(jnp.ones((breadth,), jnp.float32), RADIUS)
    offsets = [(row_off, col_off) for row_off in range(window) for col_off in range(window)]
    score_list = []
    for row_off, col_off in offsets:
        near_keys = keys_pad[row_off:row_off + height, col_off:col_off + breadth]
        inside = row_ok[row_off:row_off + height, None] * col_ok[None, col_off:col_off + breadth] > 0.5
        one_score = lax.optimization_barrier(jnp.sum(queries * near_keys, axis=-1)) * HEAD ** (-0.5)
        score_list.append(jnp.where(inside[:, :, None], one_score, -jnp.inf))
    scores = jnp.stack(score_list)
    row_max = lax.optimization_barrier(jnp.max(scores, axis=0))
    log_total = row_max + jnp.log(lax.optimization_barrier(jnp.sum(jnp.exp(scores - row_max), axis=0)))
    probability = jnp.exp(scores - log_total)
    weights = lax.optimization_barrier(probability.astype(jnp.bfloat16)).astype(jnp.float32)
    attended = jnp.zeros((height, breadth, head_count, HEAD), jnp.float32)
    for position, (row_off, col_off) in enumerate(offsets):
        near_values = values_pad[row_off:row_off + height, col_off:col_off + breadth]
        attended = attended + weights[position][..., None] * near_values
    attended = attended.reshape(height, breadth, model_width).astype(jnp.bfloat16)
    flat_up = upstream.reshape(-1, model_width)
    grad_attn = jnp.dot(flat_up, out_weight.T, preferred_element_type=jnp.float32).astype(jnp.bfloat16)
    grad_out_weight = lax.dot_general(attended.reshape(-1, model_width), flat_up, (((0,), (0,)), ((), ())), preferred_element_type=jnp.float32)
    grad_heads = lax.optimization_barrier(grad_attn).astype(jnp.float32).reshape(height, breadth, head_count, HEAD)
    grad_prob = jnp.stack([lax.optimization_barrier(jnp.sum(grad_heads * values_pad[row_off:row_off + height, col_off:col_off + breadth], axis=-1)) for row_off, col_off in offsets])
    delta_sum = lax.optimization_barrier(jnp.sum(probability * grad_prob, axis=0))
    grad_score = (probability * (grad_prob - delta_sum) * HEAD ** (-0.5)).astype(jnp.bfloat16)
    grad_score = lax.optimization_barrier(grad_score).astype(jnp.float32)
    grad_query = jnp.zeros((height, breadth, head_count, HEAD), jnp.float32)
    grad_key_pad = jnp.zeros(keys_pad.shape, jnp.float32)
    grad_value_pad = jnp.zeros(values_pad.shape, jnp.float32)
    for position, (row_off, col_off) in enumerate(offsets):
        near_keys = keys_pad[row_off:row_off + height, col_off:col_off + breadth]
        grad_query = grad_query + grad_score[position][..., None] * near_keys
        grad_key_pad = grad_key_pad.at[row_off:row_off + height, col_off:col_off + breadth].add(grad_score[position][..., None] * queries)
        grad_value_pad = grad_value_pad.at[row_off:row_off + height, col_off:col_off + breadth].add(weights[position][..., None] * grad_heads)
    grad_key = grad_key_pad[RADIUS:RADIUS + height, RADIUS:RADIUS + breadth]
    grad_value = grad_value_pad[RADIUS:RADIUS + height, RADIUS:RADIUS + breadth]
    joined = jnp.concatenate([grad_query.reshape(height, breadth, model_width), grad_key.reshape(height, breadth, model_width), grad_value.reshape(height, breadth, model_width)], axis=-1).astype(jnp.bfloat16)
    flat_joined = joined.reshape(-1, 3 * model_width)
    grad_in_weight = lax.dot_general(flat_norm, flat_joined, (((0,), (0,)), ((), ())), preferred_element_type=jnp.float32)
    grad_normed = jnp.dot(flat_joined, in_weight.T, preferred_element_type=jnp.float32).reshape(height, breadth, model_width)
    grad_gain = lax.optimization_barrier(jnp.sum(grad_normed * wide_input * inv_rms, axis=(0, 1)))
    gained = grad_normed * norm_gain
    grad_tokens = (inv_rms * (gained - wide_input * inv_rms * inv_rms * lax.optimization_barrier(jnp.mean(gained * wide_input, axis=-1, keepdims=True)))).astype(jnp.bfloat16)
    return (grad_tokens, grad_in_weight, grad_out_weight, grad_gain)

def reference(tokens, norm_gain, in_weight, out_weight, cotangent):

    def per_image(image_pair):
        return one_image(image_pair, norm_gain, in_weight, out_weight)
    grad_tokens, grad_in_weight, grad_out_weight, grad_gain = lax.map(per_image, (tokens, cotangent))
    factor = 1.0 / math.sqrt(BATCH * ROWS_ALL * COLS)
    return (grad_tokens, lax.optimization_barrier(jnp.sum(grad_in_weight, axis=0)) * factor, lax.optimization_barrier(jnp.sum(grad_out_weight, axis=0)) * factor, lax.optimization_barrier(jnp.sum(grad_gain, axis=0)) * factor)
```

```python
import math

import jax
import jax.numpy as jnp
from jax import lax
from jax.experimental import pallas as pl
from jax.experimental.pallas import tpu as pltpu
from jax.sharding import PartitionSpec as P

F32 = jnp.float32
BF16 = jnp.bfloat16
D = 256
COLS = 128
OWN = 16
FRAME = OWN + 6
PADDED = 144
NEG = -1e30
NT = (((1,), (1,)), ((), ()))
TN = (((0,), (0,)), ((), ()))


def dot(a, b, dims=(((1,), (0,)), ((), ()))):
    return lax.dot_general(a, b, dims, preferred_element_type=F32)


def attention_kernel(
    tok, up, down, cot, gain, w_in, w_out,
    gn_out, rim_up, rim_down, sums_out,
    padded, shifted, k_win, v_win, q_tiles, g_tiles, natural, attended, d_query, bias, acc, gw,
):
    here = lax.axis_index("rows")
    last = lax.axis_size("rows") - 1
    shifted[...] = jnp.zeros_like(shifted)
    gain_row = gain[...]

    def normalise(x):
        wide = x.astype(F32)
        inv = lax.rsqrt(jnp.mean(wide * wide, axis=-1, keepdims=True) + 1e-6)
        return wide * inv * gain_row

    def windows(normed, slot, frame_row):
        shifted[slot, 4 : 4 + COLS, :] = normed
        padded[frame_row] = shifted[slot].astype(BF16)
        rows = jnp.concatenate([shifted[slot, 8 * j : 8 * j + 16, :] for j in range(16)], axis=0)
        kv = dot(rows.astype(BF16), w_in[:, D:])
        k_win[frame_row] = kv[:, :D].astype(BF16).reshape(16, 16, D)
        v_win[frame_row] = kv[:, D:].astype(BF16).reshape(16, 16, D)

    def halo_row(r, carry):
        windows(normalise(up[r]), 0, r)
        windows(normalise(down[r]), 1, OWN + 3 + r)
        return carry

    def tile_order(pair):
        return [
            jnp.concatenate([pair[8 * j : 8 * j + 8], pair[COLS + 8 * j : COLS + 8 * j + 8]], axis=0)
            for j in range(16)
        ]

    def own_pair(i, carry):
        first = 2 * i
        half = i // 4
        place = pl.multiple_of((i % 4) * 16, 16)
        one = normalise(tok[first])
        two = normalise(tok[first + 1])
        windows(one, 0, first + 3)
        windows(two, 1, first + 4)
        both = jnp.concatenate([one, two], axis=0).astype(BF16)
        natural[pl.ds(first, 2)] = both.reshape(2, COLS, D)
        q = dot(both, w_in[:, :D])
        for j, tile in enumerate(tile_order(q)):
            q_tiles[half, j, pl.ds(place, 16), :] = (tile.astype(BF16).astype(F32) * 0.125).astype(BF16)
        g = dot(cot[pl.ds(first, 2)].reshape(2 * COLS, D), w_out[...], NT)
        for j, tile in enumerate(tile_order(g)):
            g_tiles[half, j, pl.ds(place, 16), :] = tile.astype(BF16)
        return carry

    lax.fori_loop(0, 3, halo_row, 0)
    lax.fori_loop(0, 8, own_pair, 0)

    key = lax.broadcasted_iota(jnp.int32, (224, D), 0)
    lane = lax.broadcasted_iota(jnp.int32, (224, D), 1)
    k_row, k_col = key // 16, key % 16
    q_row, q_col = (lane % 64) // 8, lane % 8
    near = (k_row - q_row >= 0) & (k_row - q_row <= 6) & (k_col - q_col >= 1) & (k_col - q_col <= 7)
    for half in range(2):
        if half == 0:
            inside = near & ((k_row >= 3) | (here > 0))
        else:
            inside = near & ((k_row < 11) | (here < last))
        for side in range(3):
            ok = inside
            if side == 0:
                ok = ok & (k_col >= 4)
            if side == 2:
                ok = ok & (k_col < 12)
            bias[half, side] = jnp.where(ok, 0.0, NEG)

    def zero_row(r, carry):
        acc[r] = jnp.zeros((PADDED, 2 * D), F32)
        return carry

    lax.fori_loop(0, FRAME, zero_row, 0)

    head_lane = lax.broadcasted_iota(jnp.int32, (64, D), 1) // 64

    def by_head(tile):
        return jnp.concatenate(
            [jnp.where(head_lane == h, tile, jnp.zeros_like(tile)) for h in range(4)], axis=0
        )

    def of_heads(full):
        out = full[192:256]
        for h in (2, 1, 0):
            out = jnp.where(head_lane == h, full[64 * h : 64 * h + 64], out)
        return out

    def one_tile(half, j, side):
        frame = half * 8
        k = k_win[pl.ds(frame, 14), j].reshape(224, D)
        v = v_win[pl.ds(frame, 14), j].reshape(224, D)
        q = by_head(q_tiles[half, j])
        g = by_head(g_tiles[half, j])
        s = dot(k, q, NT) + bias[half, side]
        e = jnp.exp(s - jnp.max(s, axis=0, keepdims=True))
        p = e * (1.0 / jnp.sum(e, axis=0, keepdims=True))
        weights = p.astype(BF16)
        dp = dot(v, g, NT)
        delta = jnp.sum(p * dp, axis=0, keepdims=True)
        ds = (p * (dp - delta)).astype(BF16)
        place = pl.ds(pl.multiple_of(8 * j, 8), 16)
        acc[pl.ds(frame, 14), place, :D] += dot(ds, q).reshape(14, 16, D)
        acc[pl.ds(frame, 14), place, D:] += dot(weights, g).reshape(14, 16, D)
        att = of_heads(dot(weights, v, TN))
        dq = of_heads(dot(ds, k, TN)) * 0.125
        return att.reshape(8, 8, D), dq.reshape(8, 8, D)

    def tile_pair(i, carry):
        half, jp = i // 8, i % 8
        a0, d0 = one_tile(half, 2 * jp, jnp.where(jp == 0, 0, 1))
        a1, d1 = one_tile(half, 2 * jp + 1, jnp.where(jp == 7, 2, 1))
        rows = pl.ds(half * 8, 8)
        cols = pl.ds(pl.multiple_of(16 * jp, 16), 16)
        attended[rows, cols, :] = jnp.concatenate([a0, a1], axis=1).astype(BF16)
        d_query[rows, cols, :] = jnp.concatenate([d0, d1], axis=1).astype(BF16)
        return carry

    lax.fori_loop(0, 16, tile_pair, 0)

    gw[...] = jnp.zeros_like(gw)

    def key_row(r, carry):
        both = acc[r].astype(BF16)
        gw[:, D : 3 * D] += dot(padded[r], both, TN)
        acc[r, :, :D] = dot(both, w_in[:, D:], NT)
        return carry

    lax.fori_loop(0, FRAME, key_row, 0)
    rim_up[...] = acc[0:3, 4 : 4 + COLS, :D].astype(BF16)
    rim_down[...] = acc[OWN + 3 : FRAME, 4 : 4 + COLS, :D].astype(BF16)

    def query_rows(i, carry):
        rows = pl.ds(2 * i, 2)
        dq = d_query[rows].reshape(2 * COLS, D)
        gn = dot(dq, w_in[:, :D], NT).reshape(2, COLS, D)
        gn_out[rows] = gn + acc[pl.ds(2 * i + 3, 2), 4 : 4 + COLS, :D]
        gw[:, :D] += dot(natural[rows].reshape(2 * COLS, D), dq, TN)
        gw[:, 3 * D :] += dot(
            attended[rows].reshape(2 * COLS, D), cot[rows].reshape(2 * COLS, D), TN
        )
        return carry

    lax.fori_loop(0, 8, query_rows, 0)
    for g in range(16):
        for h in range(2):
            sums_out[2 * g + h] = gw[16 * g : 16 * g + 16, 512 * h : 512 * h + 512].astype(BF16)


def attention(tok, up, down, cot, gain, w_in, w_out):
    vmem = pl.BlockSpec(memory_space=pltpu.VMEM)
    return pl.pallas_call(
        attention_kernel,
        out_shape=(
            jax.ShapeDtypeStruct((OWN, COLS, D), F32),
            jax.ShapeDtypeStruct((3, COLS, D), BF16),
            jax.ShapeDtypeStruct((3, COLS, D), BF16),
            jax.ShapeDtypeStruct((32, 16, 512), BF16),
        ),
        in_specs=[vmem] * 7,
        out_specs=(vmem,) * 4,
        scratch_shapes=[
            pltpu.VMEM((FRAME, PADDED, D), BF16),
            pltpu.VMEM((2, PADDED, D), F32),
            pltpu.VMEM((FRAME, 16, 16, D), BF16),
            pltpu.VMEM((FRAME, 16, 16, D), BF16),
            pltpu.VMEM((2, 16, 64, D), BF16),
            pltpu.VMEM((2, 16, 64, D), BF16),
            pltpu.VMEM((OWN, COLS, D), BF16),
            pltpu.VMEM((OWN, COLS, D), BF16),
            pltpu.VMEM((OWN, COLS, D), BF16),
            pltpu.VMEM((2, 3, 224, D), F32),
            pltpu.VMEM((FRAME, PADDED, 2 * D), F32),
            pltpu.VMEM((D, 4 * D), F32),
        ],
        compiler_params=pltpu.CompilerParams(vmem_limit_bytes=56 * 1024 * 1024),
        cost_estimate=pl.CostEstimate(flops=16_000_000_000, bytes_accessed=6_000_000, transcendentals=2_000_000),
    )(tok, up, down, cot, gain, w_in, w_out)


def sum_kernel(
    factor, mine, w_in, gain, g_in, g_out, g_gain,
    plane_got, z_parts, z_got, z_full, full,
    plane_send, plane_recv, z_send, z_recv, back_send, back_recv, out_send, out_recv,
):
    rows = lax.axis_index("rows")
    x = lax.axis_index("dp")
    core = rows % 2
    z = (rows // 2) % 8
    y = rows // 16
    me = (y * 4 + x) * 2 + core

    def in_plane(i):
        to_y, to_x, to_core = (y + i // 8) % 4, (x + (i // 2) % 4) % 4, (core + i % 2) % 2
        where = {"rows": (to_y * 8 + z) * 2 + to_core, "dp": to_x}
        return where, (to_y * 4 + to_x) * 2 + to_core

    def along_z(i):
        to_z = (z + i) % 8
        return {"rows": (y * 8 + to_z) * 2 + core, "dp": x}, to_z

    def remote(src, dst, send, recv, where):
        return pltpu.make_async_remote_copy(
            src_ref=src, dst_ref=dst, send_sem=send, recv_sem=recv,
            device_id=where, device_id_type=pl.DeviceIdType.MESH,
        )

    barrier = pltpu.get_barrier_semaphore()

    def greet_plane(i, carry):
        pl.semaphore_signal(barrier, inc=1, device_id=in_plane(i)[0], device_id_type=pl.DeviceIdType.MESH)
        return carry

    def greet_z(i, carry):
        pl.semaphore_signal(barrier, inc=1, device_id=along_z(i)[0], device_id_type=pl.DeviceIdType.MESH)
        return carry

    lax.fori_loop(1, 32, greet_plane, 0)
    lax.fori_loop(1, 8, greet_z, 0)
    pl.semaphore_wait(barrier, 38)

    def scatter(i):
        where, index = in_plane(i)
        return remote(mine.at[index], plane_got.at[i], plane_send.at[i], plane_recv.at[i], where)

    def z_scatter(i):
        where, index = along_z(i)
        return remote(z_parts.at[index], z_got.at[i], z_send.at[i], z_recv.at[i], where)

    def z_gather(i):
        where, index = along_z(i)
        return remote(z_full.at[z], z_full.at[z], back_send.at[i], back_recv.at[i], where)

    def gather(i):
        where, index = in_plane(i)
        return remote(full.at[me], full.at[me], out_send.at[i], out_recv.at[i], where)

    def start(make):
        def body(i, carry):
            make(i).start()
            return carry
        return body

    def wait_send(make):
        def body(i, carry):
            make(i).wait_send()
            return carry
        return body

    def wait_recv(make):
        def body(i, carry):
            make(i).wait_recv()
            return carry
        return body

    lax.fori_loop(1, 32, start(scatter), 0)

    def add_plane(i, total):
        scatter(i).wait_recv()
        return total + plane_got[i].astype(F32)

    total = lax.fori_loop(1, 32, add_plane, mine[me].astype(F32))
    for p in range(8):
        r, c = 8 * (p // 4), 128 * (p % 4)
        z_parts[p] = total[r : r + 8, c : c + 128]
    lax.fori_loop(1, 8, start(z_scatter), 0)

    def add_z(i, piece):
        z_scatter(i).wait_recv()
        return piece + z_got[i]

    z_full[z] = lax.fori_loop(1, 8, add_z, z_parts[z])
    lax.fori_loop(1, 8, start(z_gather), 0)
    lax.fori_loop(1, 8, wait_recv(z_gather), 0)
    done = jnp.concatenate(
        [jnp.concatenate([z_full[4 * a + c] for c in range(4)], axis=1) for a in range(2)], axis=0
    )
    full[me] = done.astype(BF16)
    lax.fori_loop(1, 32, start(gather), 0)
    lax.fori_loop(1, 32, wait_recv(gather), 0)
    for g in range(16):
        span = slice(16 * g, 16 * g + 16)
        left = full[2 * g].astype(F32) * factor
        right = full[2 * g + 1].astype(F32) * factor
        g_in[span, :512] = left
        g_in[span, 512:] = right[:, :256]
        g_out[span, :] = right[:, 256:]
    per_row = jnp.sum(g_in[...] * w_in[...].astype(F32), axis=1, keepdims=True)
    g_gain[...] = jnp.transpose(jnp.broadcast_to(per_row, (D, 128)))[0:1] / gain[...]
    lax.fori_loop(1, 32, wait_send(scatter), 0)
    lax.fori_loop(1, 8, wait_send(z_scatter), 0)
    lax.fori_loop(1, 8, wait_send(z_gather), 0)
    lax.fori_loop(1, 32, wait_send(gather), 0)


def sum_all(mine, w_in, gain, factor):
    vmem = pl.BlockSpec(memory_space=pltpu.VMEM)
    dma = pltpu.SemaphoreType.DMA
    return pl.pallas_call(
        lambda *refs: sum_kernel(factor, *refs),
        out_shape=(
            jax.ShapeDtypeStruct((D, 3 * D), F32),
            jax.ShapeDtypeStruct((D, D), F32),
            jax.ShapeDtypeStruct((1, D), F32),
        ),
        in_specs=[vmem] * 3,
        out_specs=(vmem,) * 3,
        scratch_shapes=[
            pltpu.VMEM((32, 16, 512), BF16),
            pltpu.VMEM((8, 8, 128), F32),
            pltpu.VMEM((8, 8, 128), F32),
            pltpu.VMEM((8, 8, 128), F32),
            pltpu.VMEM((32, 16, 512), BF16),
            dma((32,)), dma((32,)), dma((8,)), dma((8,)),
            dma((8,)), dma((8,)), dma((32,)), dma((32,)),
        ],
        compiler_params=pltpu.CompilerParams(
            collective_id=0, has_side_effects=True, vmem_limit_bytes=32 * 1024 * 1024
        ),
    )(mine, w_in, gain)


def halo(first, final):
    count = lax.axis_size("rows")
    from_left = lax.ppermute(final, "rows", [(i, i + 1) for i in range(count - 1)])
    from_right = lax.ppermute(first, "rows", [(i + 1, i) for i in range(count - 1)])
    return from_left, from_right


def local(tokens, norm_gain, in_weight, out_weight, cotangent):
    tok = tokens[0]
    gain = norm_gain.reshape(1, D)
    up, down = halo(tok[:3], tok[-3:])
    gn, rim_up, rim_down, mine = attention(tok, up, down, cotangent[0], gain, in_weight, out_weight)
    add_top, add_bottom = halo(rim_up, rim_down)
    factor = 1.0 / math.sqrt(lax.axis_size("rows") * lax.axis_size("dp") * OWN * COLS)
    g_in, g_out, g_gain = sum_all(mine, in_weight, gain, factor)
    wide = tok.astype(F32)
    inv = lax.rsqrt(jnp.mean(wide * wide, axis=-1, keepdims=True) + 1e-6)
    gn = gn.at[:3].add(add_top.astype(F32)).at[-3:].add(add_bottom.astype(F32))
    gained = gn * norm_gain
    grad_tokens = inv * (gained - wide * inv * inv * jnp.mean(gained * wide, axis=-1, keepdims=True))
    return grad_tokens.astype(BF16)[None], g_in, g_out, g_gain.reshape(D)


def solution(mesh):
    return jax.shard_map(
        local,
        mesh=mesh,
        in_specs=(P("dp", "rows", None, None), P(), P(), P(), P("dp", "rows", None, None)),
        out_specs=(P("dp", "rows", None, None), P(), P(), P()),
        check_vma=False,
    )
```

```python
import math
from types import SimpleNamespace

import jax
import jax.numpy as jnp
from jax import lax
from jax.experimental import pallas as pl
from jax.experimental.pallas import tpu as pltpu
from jax.sharding import PartitionSpec as P

F32 = jnp.float32
BF16 = jnp.bfloat16
D = 256
COLS = 128
OWN = 16
FRAME = OWN + 6
PADDED = 144
NEG = -1e30
NT = (((1,), (1,)), ((), ()))
TN = (((0,), (0,)), ((), ()))
VMEM_BYTES = 58 * 1024 * 1024

BUFFERS = {
    "halo": ((2, 3, COLS, D), BF16),
    "shifted": ((2, PADDED, D), F32),
    "normed": ((FRAME, COLS, D), BF16),
    "k_win": ((FRAME, 16, 16, D), BF16),
    "v_win": ((FRAME, 16, 16, D), BF16),
    "q_tiles": ((2, 16, 64, D), BF16),
    "g_tiles": ((2, 16, 64, D), BF16),
    "attended": ((OWN, COLS, D), BF16),
    "joined": ((FRAME, COLS, 3 * D), BF16),
    "bias": ((2, 3, 224, D), F32),
    "acc": ((FRAME, PADDED, 2 * D), F32),
    "gn": ((OWN, COLS, D), F32),
    "sums": ((32, 16, 512), BF16),
    "rim_out": ((2, 3, COLS, D), BF16),
    "rim_in": ((2, 3, COLS, D), BF16),
}


def dot(a, b, dims=(((1,), (0,)), ((), ()))):
    return lax.dot_general(a, b, dims, preferred_element_type=F32)


def inverse_rms(wide):
    return lax.rsqrt(jnp.mean(wide * wide, axis=-1, keepdims=True) + 1e-6)


def windows(b, x, slot, frame_row):
    wide = x.astype(F32)
    normed = wide * inverse_rms(wide) * b.gain[...]
    b.normed[frame_row] = normed.astype(BF16)
    b.shifted[slot, 4 : 4 + COLS, :] = normed
    rows = jnp.concatenate([b.shifted[slot, 8 * j : 8 * j + 16, :] for j in range(16)], axis=0)
    kv = dot(rows.astype(BF16), b.w_in[:, D:])
    b.k_win[frame_row] = kv[:, :D].astype(BF16).reshape(16, 16, D)
    b.v_win[frame_row] = kv[:, D:].astype(BF16).reshape(16, 16, D)


def clear(b):
    b.shifted[...] = jnp.zeros_like(b.shifted)
    for r in range(3):
        b.joined[r, :, :D] = jnp.zeros((COLS, D), BF16)
        b.joined[OWN + 3 + r, :, :D] = jnp.zeros((COLS, D), BF16)

    def zero_row(r, carry):
        b.acc[r] = jnp.zeros((PADDED, 2 * D), F32)
        return carry

    lax.fori_loop(0, FRAME, zero_row, 0)


def mask(b, here, last):
    key = lax.broadcasted_iota(jnp.int32, (224, D), 0)
    lane = lax.broadcasted_iota(jnp.int32, (224, D), 1)
    k_row, k_col = key // 16, key % 16
    q_row, q_col = (lane % 64) // 8, lane % 8
    near = (k_row - q_row >= 0) & (k_row - q_row <= 6) & (k_col - q_col >= 1) & (k_col - q_col <= 7)
    for half in range(2):
        if half == 0:
            inside = near & ((k_row >= 3) | (here > 0))
        else:
            inside = near & ((k_row < 11) | (here < last))
        for side in range(3):
            ok = inside
            if side == 0:
                ok = ok & (k_col >= 4)
            if side == 2:
                ok = ok & (k_col < 12)
            b.bias[half, side] = jnp.where(ok, 0.0, NEG)


def own_rows(b):
    def tile_order(pair):
        return [
            jnp.concatenate([pair[8 * j : 8 * j + 8], pair[COLS + 8 * j : COLS + 8 * j + 8]], axis=0)
            for j in range(16)
        ]

    def own_pair(i, carry):
        first = 2 * i
        half = i // 4
        place = pl.multiple_of((i % 4) * 16, 16)
        windows(b, b.tok[first], 0, first + 3)
        windows(b, b.tok[first + 1], 1, first + 4)
        both = b.normed[pl.ds(first + 3, 2)].reshape(2 * COLS, D)
        q = dot(both, b.w_in[:, :D])
        for j, tile in enumerate(tile_order(q)):
            b.q_tiles[half, j, pl.ds(place, 16), :] = (tile.astype(BF16).astype(F32) * 0.125).astype(BF16)
        g = dot(b.cot[pl.ds(first, 2)].reshape(2 * COLS, D), b.w_out[...], NT)
        for j, tile in enumerate(tile_order(g)):
            b.g_tiles[half, j, pl.ds(place, 16), :] = tile.astype(BF16)
        return carry

    lax.fori_loop(0, 8, own_pair, 0)


def halo_rows(b):
    def halo_row(r, carry):
        windows(b, b.halo[0, r], 0, r)
        windows(b, b.halo[1, r], 1, OWN + 3 + r)
        return carry

    lax.fori_loop(0, 3, halo_row, 0)


def attend(b):
    head_lane = lax.broadcasted_iota(jnp.int32, (64, D), 1) // 64

    def by_head(tile):
        return jnp.concatenate(
            [jnp.where(head_lane == h, tile, jnp.zeros_like(tile)) for h in range(4)], axis=0
        )

    def of_heads(full):
        out = full[192:256]
        for h in (2, 1, 0):
            out = jnp.where(head_lane == h, full[64 * h : 64 * h + 64], out)
        return out

    def one_tile(half, j, side):
        frame = half * 8
        k = b.k_win[pl.ds(frame, 14), j].reshape(224, D)
        v = b.v_win[pl.ds(frame, 14), j].reshape(224, D)
        q = by_head(b.q_tiles[half, j])
        g = by_head(b.g_tiles[half, j])
        s = dot(k, q, NT) + b.bias[half, side]
        e = jnp.exp(s - jnp.max(s, axis=0, keepdims=True))
        p = e * (1.0 / jnp.sum(e, axis=0, keepdims=True))
        weights = p.astype(BF16)
        dp = dot(v, g, NT)
        delta = jnp.sum(p * dp, axis=0, keepdims=True)
        ds = (p * (dp - delta)).astype(BF16)
        place = pl.ds(pl.multiple_of(8 * j, 8), 16)
        b.acc[pl.ds(frame, 14), place, :D] += dot(ds, q).reshape(14, 16, D)
        b.acc[pl.ds(frame, 14), place, D:] += dot(weights, g).reshape(14, 16, D)
        att = of_heads(dot(weights, v, TN))
        dq = of_heads(dot(ds, k, TN)) * 0.125
        return att.reshape(8, 8, D), dq.reshape(8, 8, D)

    def tile_pair(i, carry):
        half, jp = i // 8, i % 8
        a0, d0 = one_tile(half, 2 * jp, jnp.where(jp == 0, 0, 1))
        a1, d1 = one_tile(half, 2 * jp + 1, jnp.where(jp == 7, 2, 1))
        cols = pl.ds(pl.multiple_of(16 * jp, 16), 16)
        b.attended[pl.ds(half * 8, 8), cols, :] = jnp.concatenate([a0, a1], axis=1).astype(BF16)
        b.joined[pl.ds(half * 8 + 3, 8), cols, :D] = jnp.concatenate([d0, d1], axis=1).astype(BF16)
        return carry

    lax.fori_loop(0, 16, tile_pair, 0)


def weight_sums(b):
    def key_row(r, carry):
        b.joined[r, :, D:] = b.acc[r, 4 : 4 + COLS, :].astype(BF16)
        return carry

    lax.fori_loop(0, FRAME, key_row, 0)
    g_in = dot(b.normed[...].reshape(FRAME * COLS, D), b.joined[...].reshape(FRAME * COLS, 3 * D), TN)
    g_out = dot(b.attended[...].reshape(OWN * COLS, D), b.cot[...].reshape(OWN * COLS, D), TN)
    for g in range(16):
        span = slice(16 * g, 16 * g + 16)
        b.sums[2 * g] = g_in[span, :512].astype(BF16)
        b.sums[2 * g + 1] = jnp.concatenate([g_in[span, 512:], g_out[span]], axis=1).astype(BF16)


def rim_rows(b):
    for side, first in ((0, 0), (1, OWN + 3)):
        rows = b.joined[first : first + 3].reshape(3 * COLS, 3 * D)
        b.rim_out[side] = dot(rows, b.w_in[...], NT).reshape(3, COLS, D).astype(BF16)


def own_gn(b):
    def four(i, carry):
        rows = b.joined[pl.ds(3 + 4 * i, 4)].reshape(4 * COLS, 3 * D)
        b.gn[pl.ds(4 * i, 4)] = dot(rows, b.w_in[...], NT).reshape(4, COLS, D)
        return carry

    lax.fori_loop(0, 4, four, 0)


def finish(b, row, rim=None):
    wide = b.tok[row].astype(F32)
    inv = inverse_rms(wide)
    gn = b.gn[row]
    if rim is not None:
        gn = gn + rim.astype(F32)
    gained = gn * b.gain[...]
    mean = jnp.mean(gained * wide, axis=-1, keepdims=True)
    b.gt[row] = (inv * (gained - wide * (inv * inv * mean))).astype(BF16)


def finish_rows(b, low, high):
    def body(r, carry):
        finish(b, r)
        return carry

    lax.fori_loop(low, high, body, 0)


def block_kernel(factor, names, *refs):
    b = SimpleNamespace(**dict(zip(names, refs)))
    rows = lax.axis_index("rows")
    count = lax.axis_size("rows")
    x = lax.axis_index("dp")
    core = rows % 2
    z = (rows // 2) % 8
    y = rows // 16
    me = (y * 4 + x) * 2 + core
    before = {"rows": (rows + count - 1) % count, "dp": x}
    after = {"rows": (rows + 1) % count, "dp": x}

    def in_plane(i):
        to_y, to_x, to_core = (y + i // 8) % 4, (x + (i // 2) % 4) % 4, (core + i % 2) % 2
        where = {"rows": (to_y * 8 + z) * 2 + to_core, "dp": to_x}
        return where, (to_y * 4 + to_x) * 2 + to_core

    def along_z(i):
        to_z = (z + i) % 8
        return {"rows": (y * 8 + to_z) * 2 + core, "dp": x}, to_z

    def remote(src, dst, send, recv, where):
        return pltpu.make_async_remote_copy(
            src_ref=src, dst_ref=dst, send_sem=send, recv_sem=recv,
            device_id=where, device_id_type=pl.DeviceIdType.MESH,
        )

    barrier = pltpu.get_barrier_semaphore()

    def greet(where):
        pl.semaphore_signal(barrier, inc=1, device_id=where, device_id_type=pl.DeviceIdType.MESH)

    def greet_plane(i, carry):
        greet(in_plane(i)[0])
        return carry

    def greet_z(i, carry):
        greet(along_z(i)[0])
        return carry

    greet(before)
    greet(after)
    lax.fori_loop(1, 32, greet_plane, 0)
    lax.fori_loop(1, 8, greet_z, 0)
    clear(b)
    pl.semaphore_wait(barrier, 40)

    def halo_copies():
        return (
            remote(b.tok.at[pl.ds(OWN - 3, 3)], b.halo.at[0], b.near_send.at[0], b.near_recv.at[0], after),
            remote(b.tok.at[pl.ds(0, 3)], b.halo.at[1], b.near_send.at[1], b.near_recv.at[1], before),
        )

    def rim_copies():
        return (
            remote(b.rim_out.at[0], b.rim_in.at[1], b.near_send.at[2], b.near_recv.at[2], before),
            remote(b.rim_out.at[1], b.rim_in.at[0], b.near_send.at[3], b.near_recv.at[3], after),
        )

    def scatter(i):
        where, index = in_plane(i)
        return remote(b.sums.at[index], b.plane_got.at[i], b.plane_send.at[i], b.plane_recv.at[i], where)

    def z_scatter(i):
        where, index = along_z(i)
        return remote(b.z_parts.at[index], b.z_got.at[i], b.z_send.at[i], b.z_recv.at[i], where)

    def z_gather(i):
        where, index = along_z(i)
        return remote(b.z_full.at[z], b.z_full.at[z], b.back_send.at[i], b.back_recv.at[i], where)

    def gather(i):
        where, index = in_plane(i)
        return remote(b.full.at[me], b.full.at[me], b.out_send.at[i], b.out_recv.at[i], where)

    def each(make, high, act):
        def body(i, carry):
            act(make(i))
            return carry

        lax.fori_loop(1, high, body, 0)

    def start(copy):
        copy.start()

    def wait_send(copy):
        copy.wait_send()

    def wait_recv(copy):
        copy.wait_recv()

    for copy in halo_copies():
        copy.start()
    mask(b, rows, count - 1)
    own_rows(b)
    for copy in halo_copies():
        copy.wait_recv()
    halo_rows(b)
    attend(b)
    weight_sums(b)
    each(scatter, 32, start)
    rim_rows(b)
    for copy in rim_copies():
        copy.start()
    own_gn(b)

    def add_plane(i, total):
        scatter(i).wait_recv()
        return total + b.plane_got[i].astype(F32)

    total = lax.fori_loop(1, 32, add_plane, b.sums[me].astype(F32))
    for p in range(8):
        r, c = 8 * (p // 4), 128 * (p % 4)
        b.z_parts[p] = total[r : r + 8, c : c + 128]
    each(z_scatter, 8, start)
    finish_rows(b, 3, 8)

    def add_z(i, piece):
        z_scatter(i).wait_recv()
        return piece + b.z_got[i]

    b.z_full[z] = lax.fori_loop(1, 8, add_z, b.z_parts[z])
    each(z_gather, 8, start)
    finish_rows(b, 8, 13)
    each(z_gather, 8, wait_recv)
    done = jnp.concatenate(
        [jnp.concatenate([b.z_full[4 * a + c] for c in range(4)], axis=1) for a in range(2)], axis=0
    )
    b.full[me] = done.astype(BF16)
    each(gather, 32, start)
    for copy in rim_copies():
        copy.wait_recv()

    def edge(r, carry):
        finish(b, r, b.rim_in[0, r])
        finish(b, OWN - 3 + r, b.rim_in[1, r])
        return carry

    lax.fori_loop(0, 3, edge, 0)
    each(gather, 32, wait_recv)
    for g in range(16):
        span = slice(16 * g, 16 * g + 16)
        left = b.full[2 * g].astype(F32) * factor
        right = b.full[2 * g + 1].astype(F32) * factor
        b.g_in[span, :512] = left
        b.g_in[span, 512:] = right[:, :256]
        b.g_out[span, :] = right[:, 256:]
    per_row = jnp.sum(b.g_in[...] * b.w_in[...].astype(F32), axis=1, keepdims=True)
    b.g_gain[...] = jnp.transpose(jnp.broadcast_to(per_row, (D, 128)))[0:1] / b.gain[...]
    for copy in halo_copies() + rim_copies():
        copy.wait_send()
    each(scatter, 32, wait_send)
    each(z_scatter, 8, wait_send)
    each(z_gather, 8, wait_send)
    each(gather, 32, wait_send)


def block(tok, cot, gain, w_in, w_out, factor):
    vmem = pl.BlockSpec(memory_space=pltpu.VMEM)
    dma = pltpu.SemaphoreType.DMA
    outs = {
        "gt": ((OWN, COLS, D), BF16),
        "g_in": ((D, 3 * D), F32),
        "g_out": ((D, D), F32),
        "g_gain": ((1, D), F32),
    }
    slots = {
        "plane_got": ((32, 16, 512), BF16),
        "z_parts": ((8, 8, 128), F32),
        "z_got": ((8, 8, 128), F32),
        "z_full": ((8, 8, 128), F32),
        "full": ((32, 16, 512), BF16),
    }
    sems = {
        "near_send": 4, "near_recv": 4, "plane_send": 32, "plane_recv": 32, "z_send": 8, "z_recv": 8,
        "back_send": 8, "back_recv": 8, "out_send": 32, "out_recv": 32,
    }
    names = ["tok", "cot", "gain", "w_in", "w_out", *outs, *BUFFERS, *slots, *sems]

    def kernel(*refs):
        block_kernel(factor, names, *refs)

    return pl.pallas_call(
        kernel,
        out_shape=tuple(jax.ShapeDtypeStruct(*o) for o in outs.values()),
        in_specs=[vmem] * 5,
        out_specs=(vmem,) * 4,
        scratch_shapes=[
            *(pltpu.VMEM(*s) for s in BUFFERS.values()),
            *(pltpu.VMEM(*s) for s in slots.values()),
            *(dma((n,)) for n in sems.values()),
        ],
        compiler_params=pltpu.CompilerParams(
            collective_id=0, has_side_effects=True, vmem_limit_bytes=VMEM_BYTES
        ),
    )(tok, cot, gain, w_in, w_out)


def local(tokens, norm_gain, in_weight, out_weight, cotangent):
    factor = 1.0 / math.sqrt(lax.axis_size("rows") * lax.axis_size("dp") * OWN * COLS)
    gt, g_in, g_out, g_gain = block(
        tokens[0], cotangent[0], norm_gain.reshape(1, D), in_weight, out_weight, factor
    )
    return gt[None], g_in, g_out, g_gain.reshape(D)


def solution(mesh):
    return jax.shard_map(
        local,
        mesh=mesh,
        in_specs=(P("dp", "rows", None, None), P(), P(), P(), P("dp", "rows", None, None)),
        out_specs=(P("dp", "rows", None, None), P(), P(), P()),
        check_vma=False,
    )
```

```python
import math
from types import SimpleNamespace

import jax
import jax.numpy as jnp
from jax import lax
from jax.experimental import pallas as pl
from jax.experimental.pallas import tpu as pltpu
from jax.sharding import PartitionSpec as P

F32 = jnp.float32
BF16 = jnp.bfloat16
D = 256
COLS = 128
OWN = 16
FRAME = OWN + 6
PADDED = 144
NEG = -1e30
NT = (((1,), (1,)), ((), ()))
TN = (((0,), (0,)), ((), ()))
VMEM_BYTES = 58 * 1024 * 1024

BUFFERS = {
    "halo": ((2, 3, COLS, D), BF16),
    "shifted": ((2, PADDED, D), F32),
    "normed": ((FRAME, COLS, D), BF16),
    "k_win": ((FRAME, 16, 16, D), BF16),
    "v_win": ((FRAME, 16, 16, D), BF16),
    "q_tiles": ((2, 16, 64, D), BF16),
    "g_tiles": ((2, 16, 64, D), BF16),
    "attended": ((OWN, COLS, D), BF16),
    "joined": ((FRAME, COLS, 3 * D), BF16),
    "bias": ((2, 3, 224, D), F32),
    "acc": ((FRAME, PADDED, 2 * D), F32),
    "gn": ((OWN, COLS, D), F32),
    "sums": ((32, 16, 512), BF16),
    "rim_out": ((2, 3, COLS, D), BF16),
    "rim_in": ((2, 3, COLS, D), BF16),
}


def dot(a, b, dims=(((1,), (0,)), ((), ()))):
    return lax.dot_general(a, b, dims, preferred_element_type=F32)


def inverse_rms(wide):
    return lax.rsqrt(jnp.mean(wide * wide, axis=-1, keepdims=True) + 1e-6)


def windows(b, x, slot, frame_row):
    wide = x.astype(F32)
    normed = wide * inverse_rms(wide) * b.gain[...]
    b.normed[frame_row] = normed.astype(BF16)
    b.shifted[slot, 4 : 4 + COLS, :] = normed
    rows = jnp.concatenate([b.shifted[slot, 8 * j : 8 * j + 16, :] for j in range(16)], axis=0)
    kv = dot(rows.astype(BF16), b.w_in[:, D:])
    b.k_win[frame_row] = kv[:, :D].astype(BF16).reshape(16, 16, D)
    b.v_win[frame_row] = kv[:, D:].astype(BF16).reshape(16, 16, D)


def clear(b):
    b.shifted[...] = jnp.zeros_like(b.shifted)
    for r in range(3):
        b.joined[r, :, :D] = jnp.zeros((COLS, D), BF16)
        b.joined[OWN + 3 + r, :, :D] = jnp.zeros((COLS, D), BF16)

    def zero_row(r, carry):
        b.acc[r] = jnp.zeros((PADDED, 2 * D), F32)
        return carry

    lax.fori_loop(0, FRAME, zero_row, 0)


def mask(b, here, last):
    key = lax.broadcasted_iota(jnp.int32, (224, D), 0)
    lane = lax.broadcasted_iota(jnp.int32, (224, D), 1)
    k_row, k_col = key // 16, key % 16
    q_row, q_col = (lane % 64) // 8, lane % 8
    near = (k_row - q_row >= 0) & (k_row - q_row <= 6) & (k_col - q_col >= 1) & (k_col - q_col <= 7)
    for half in range(2):
        if half == 0:
            inside = near & ((k_row >= 3) | (here > 0))
        else:
            inside = near & ((k_row < 11) | (here < last))
        for side in range(3):
            ok = inside
            if side == 0:
                ok = ok & (k_col >= 4)
            if side == 2:
                ok = ok & (k_col < 12)
            b.bias[half, side] = jnp.where(ok, 0.0, NEG)


def own_rows(b):
    def tile_order(pair):
        return [
            jnp.concatenate([pair[8 * j : 8 * j + 8], pair[COLS + 8 * j : COLS + 8 * j + 8]], axis=0)
            for j in range(16)
        ]

    def own_pair(i, carry):
        first = 2 * i
        half = i // 4
        place = pl.multiple_of((i % 4) * 16, 16)
        windows(b, b.tok[first], 0, first + 3)
        windows(b, b.tok[first + 1], 1, first + 4)
        both = b.normed[pl.ds(first + 3, 2)].reshape(2 * COLS, D)
        q = dot(both, b.w_in[:, :D])
        for j, tile in enumerate(tile_order(q)):
            b.q_tiles[half, j, pl.ds(place, 16), :] = (tile.astype(BF16).astype(F32) * 0.125).astype(BF16)
        g = dot(b.cot[pl.ds(first, 2)].reshape(2 * COLS, D), b.w_out[...], NT)
        for j, tile in enumerate(tile_order(g)):
            b.g_tiles[half, j, pl.ds(place, 16), :] = tile.astype(BF16)
        return carry

    lax.fori_loop(0, 8, own_pair, 0)


def halo_rows(b):
    def halo_row(r, carry):
        windows(b, b.halo[0, r], 0, r)
        windows(b, b.halo[1, r], 1, OWN + 3 + r)
        return carry

    lax.fori_loop(0, 3, halo_row, 0)


def attend(b):
    head_lane = lax.broadcasted_iota(jnp.int32, (64, D), 1) // 64

    def by_head(tile):
        return jnp.concatenate(
            [jnp.where(head_lane == h, tile, jnp.zeros_like(tile)) for h in range(4)], axis=0
        )

    def of_heads(full):
        out = full[192:256]
        for h in (2, 1, 0):
            out = jnp.where(head_lane == h, full[64 * h : 64 * h + 64], out)
        return out

    def one_tile(half, j, side):
        frame = half * 8
        k = b.k_win[pl.ds(frame, 14), j].reshape(224, D)
        v = b.v_win[pl.ds(frame, 14), j].reshape(224, D)
        q = by_head(b.q_tiles[half, j])
        g = by_head(b.g_tiles[half, j])
        s = dot(k, q, NT) + b.bias[half, side]
        e = jnp.exp(s - jnp.max(s, axis=0, keepdims=True))
        p = e * (1.0 / jnp.sum(e, axis=0, keepdims=True))
        weights = p.astype(BF16)
        dp = dot(v, g, NT)
        delta = jnp.sum(p * dp, axis=0, keepdims=True)
        ds = (p * (dp - delta)).astype(BF16)
        place = pl.ds(pl.multiple_of(8 * j, 8), 16)
        b.acc[pl.ds(frame, 14), place, :D] += dot(ds, q).reshape(14, 16, D)
        b.acc[pl.ds(frame, 14), place, D:] += dot(weights, g).reshape(14, 16, D)
        att = of_heads(dot(weights, v, TN))
        dq = of_heads(dot(ds, k, TN)) * 0.125
        return att.reshape(8, 8, D), dq.reshape(8, 8, D)

    def tile_pair(i, carry):
        one_pair(0, i)
        one_pair(1, i)
        return carry

    def one_pair(half, jp):
        a0, d0 = one_tile(half, 2 * jp, jnp.where(jp == 0, 0, 1))
        a1, d1 = one_tile(half, 2 * jp + 1, jnp.where(jp == 7, 2, 1))
        cols = pl.ds(pl.multiple_of(16 * jp, 16), 16)
        b.attended[pl.ds(half * 8, 8), cols, :] = jnp.concatenate([a0, a1], axis=1).astype(BF16)
        b.joined[pl.ds(half * 8 + 3, 8), cols, :D] = jnp.concatenate([d0, d1], axis=1).astype(BF16)

    lax.fori_loop(0, 8, tile_pair, 0)


def weight_sums(b):
    def key_row(r, carry):
        b.joined[r, :, D:] = b.acc[r, 4 : 4 + COLS, :].astype(BF16)
        return carry

    lax.fori_loop(0, FRAME, key_row, 0)
    g_in = dot(b.normed[...].reshape(FRAME * COLS, D), b.joined[...].reshape(FRAME * COLS, 3 * D), TN)
    g_out = dot(b.attended[...].reshape(OWN * COLS, D), b.cot[...].reshape(OWN * COLS, D), TN)
    for g in range(16):
        span = slice(16 * g, 16 * g + 16)
        b.sums[2 * g] = g_in[span, :512].astype(BF16)
        b.sums[2 * g + 1] = jnp.concatenate([g_in[span, 512:], g_out[span]], axis=1).astype(BF16)


def rim_rows(b):
    for side, first in ((0, 0), (1, OWN + 3)):
        rows = b.joined[first : first + 3].reshape(3 * COLS, 3 * D)
        b.rim_out[side] = dot(rows, b.w_in[...], NT).reshape(3, COLS, D).astype(BF16)


def own_gn(b):
    def four(i, carry):
        rows = b.joined[pl.ds(3 + 4 * i, 4)].reshape(4 * COLS, 3 * D)
        b.gn[pl.ds(4 * i, 4)] = dot(rows, b.w_in[...], NT).reshape(4, COLS, D)
        return carry

    lax.fori_loop(0, 4, four, 0)


def finish(b, row, rim=None):
    wide = b.tok[row].astype(F32)
    inv = inverse_rms(wide)
    gn = b.gn[row]
    if rim is not None:
        gn = gn + rim.astype(F32)
    gained = gn * b.gain[...]
    mean = jnp.mean(gained * wide, axis=-1, keepdims=True)
    b.gt[row] = (inv * (gained - wide * (inv * inv * mean))).astype(BF16)


def finish_rows(b, low, high):
    def body(r, carry):
        finish(b, r)
        return carry

    lax.fori_loop(low, high, body, 0)


def block_kernel(names, *refs):
    b = SimpleNamespace(**dict(zip(names, refs)))
    rows = lax.axis_index("rows")
    count = lax.axis_size("rows")
    x = lax.axis_index("dp")
    core = rows % 2
    z = (rows // 2) % 8
    y = rows // 16
    me = y * 4 + x
    before = {"rows": (rows + count - 1) % count, "dp": x}
    after = {"rows": (rows + 1) % count, "dp": x}
    partner = {"rows": rows + 1 - 2 * core, "dp": x}
    mine = 16 * core
    other = 16 - mine

    def in_plane(i):
        to_y, to_x = (y + i // 4) % 4, (x + i % 4) % 4
        return {"rows": (to_y * 8 + z) * 2 + core, "dp": to_x}, to_y * 4 + to_x

    def from_plane(i):
        return ((y + 4 - i // 4) % 4) * 4 + (x + 4 - i % 4) % 4

    def along_z(i):
        return {"rows": (y * 8 + (z + i) % 8) * 2 + core, "dp": x}

    def remote(src, dst, send, recv, where):
        return pltpu.make_async_remote_copy(
            src_ref=src, dst_ref=dst, send_sem=send, recv_sem=recv,
            device_id=where, device_id_type=pl.DeviceIdType.MESH,
        )

    barrier = pltpu.get_barrier_semaphore()

    def greet(where):
        pl.semaphore_signal(barrier, inc=1, device_id=where, device_id_type=pl.DeviceIdType.MESH)

    def greet_plane(i, carry):
        greet(in_plane(i)[0])
        return carry

    def greet_z(i, carry):
        greet(along_z(i))
        return carry

    greet(before)
    greet(after)
    greet(partner)
    lax.fori_loop(1, 16, greet_plane, 0)
    lax.fori_loop(1, 8, greet_z, 0)
    clear(b)
    pl.semaphore_wait(barrier, 25)

    def halo_copies():
        return (
            remote(b.tok.at[pl.ds(OWN - 3, 3)], b.halo.at[0], b.near_send.at[0], b.near_recv.at[0], after),
            remote(b.tok.at[pl.ds(0, 3)], b.halo.at[1], b.near_send.at[1], b.near_recv.at[1], before),
        )

    def rim_copies():
        return (
            remote(b.rim_out.at[0], b.rim_in.at[1], b.near_send.at[2], b.near_recv.at[2], before),
            remote(b.rim_out.at[1], b.rim_in.at[0], b.near_send.at[3], b.near_recv.at[3], after),
        )

    def core_scatter(i):
        place = in_plane(i)[1]
        return remote(b.sums.at[other + place], b.core_got.at[i], b.core_send.at[i], b.core_recv.at[i], partner)

    def scatter(i):
        where, place = in_plane(i)
        return remote(b.paired.at[i], b.plane_got.at[i], b.plane_send.at[i], b.plane_recv.at[i], where)

    def z_share(i):
        where = along_z(i)
        return remote(b.z_all.at[z], b.z_all.at[z], b.z_send.at[i], b.z_recv.at[i], where)

    def gather(i):
        where, place = in_plane(i)
        return remote(b.full.at[mine + me], b.full.at[mine + me], b.out_send.at[i], b.out_recv.at[i], where)

    def core_gather(i):
        chunk = b.full.at[mine + from_plane(i)]
        return remote(chunk, chunk, b.last_send.at[i], b.last_recv.at[i], partner)

    def each(make, low, high, act):
        def body(i, carry):
            act(make(i))
            return carry

        lax.fori_loop(low, high, body, 0)

    def start(copy):
        copy.start()

    def wait_send(copy):
        copy.wait_send()

    def wait_recv(copy):
        copy.wait_recv()

    for copy in halo_copies():
        copy.start()
    mask(b, rows, count - 1)
    own_rows(b)
    for copy in halo_copies():
        copy.wait_recv()
    halo_rows(b)
    attend(b)
    weight_sums(b)
    each(core_scatter, 1, 16, start)
    core_scatter(0).start()
    rim_rows(b)
    for copy in rim_copies():
        copy.start()

    def pair(i):
        core_scatter(i).wait_recv()
        return b.sums[mine + in_plane(i)[1]].astype(F32) + b.core_got[i].astype(F32)

    def pair_and_send(i, carry):
        b.paired[i] = pair(i).astype(BF16)
        scatter(i).start()
        return carry

    lax.fori_loop(1, 16, pair_and_send, 0)
    own_gn(b)

    def add_plane(i, total):
        scatter(i).wait_recv()
        return total + b.plane_got[i].astype(F32)

    total = lax.fori_loop(1, 16, add_plane, pair(0))
    b.z_all[z] = total.astype(BF16)
    each(z_share, 1, 8, start)
    finish_rows(b, 3, 13)
    each(z_share, 1, 8, wait_recv)
    whole = b.z_all[0].astype(F32)
    for i in range(1, 8):
        whole = whole + b.z_all[i].astype(F32)
    b.full[mine + me] = whole.astype(BF16)
    each(gather, 1, 16, start)
    core_gather(0).start()
    for copy in rim_copies():
        copy.wait_recv()

    def edge(r, carry):
        finish(b, r, b.rim_in[0, r])
        finish(b, OWN - 3 + r, b.rim_in[1, r])
        return carry

    lax.fori_loop(0, 3, edge, 0)

    def pass_on(i, carry):
        gather(i).wait_recv()
        core_gather(i).start()
        return carry

    lax.fori_loop(1, 16, pass_on, 0)
    each(core_gather, 0, 16, wait_recv)
    for copy in halo_copies() + rim_copies():
        copy.wait_send()
    each(core_scatter, 0, 16, wait_send)
    each(scatter, 1, 16, wait_send)
    each(z_share, 1, 8, wait_send)
    each(gather, 1, 16, wait_send)
    each(core_gather, 0, 16, wait_send)


def block(tok, cot, gain, w_in, w_out):
    vmem = pl.BlockSpec(memory_space=pltpu.VMEM)
    dma = pltpu.SemaphoreType.DMA
    outs = {"gt": ((OWN, COLS, D), BF16), "full": ((32, 16, 512), BF16)}
    slots = {
        "core_got": ((16, 16, 512), BF16),
        "paired": ((16, 16, 512), BF16),
        "plane_got": ((16, 16, 512), BF16),
        "z_all": ((8, 16, 512), BF16),
    }
    sems = {
        "near_send": 4, "near_recv": 4, "core_send": 16, "core_recv": 16, "plane_send": 16, "plane_recv": 16,
        "z_send": 8, "z_recv": 8, "out_send": 16, "out_recv": 16,
        "last_send": 16, "last_recv": 16,
    }
    names = ["tok", "cot", "gain", "w_in", "w_out", *outs, *BUFFERS, *slots, *sems]

    def kernel(*refs):
        block_kernel(names, *refs)

    return pl.pallas_call(
        kernel,
        out_shape=tuple(jax.ShapeDtypeStruct(*o) for o in outs.values()),
        in_specs=[vmem] * 5,
        out_specs=(vmem,) * 2,
        scratch_shapes=[
            *(pltpu.VMEM(*s) for s in BUFFERS.values()),
            *(pltpu.VMEM(*s) for s in slots.values()),
            *(dma((n,)) for n in sems.values()),
        ],
        compiler_params=pltpu.CompilerParams(
            collective_id=0, has_side_effects=True, vmem_limit_bytes=VMEM_BYTES
        ),
    )(tok, cot, gain, w_in, w_out)


def outputs(gt, full, gain, w_in, factor):
    def kernel(gt_ref, full_hbm, gain_ref, w_ref, gt_out, g_in, g_out, g_gain, full_ref, sem):
        copy = pltpu.make_async_copy(gt_ref, gt_out, sem.at[0])
        copy.start()
        fetch = pltpu.make_async_copy(full_hbm, full_ref, sem.at[1])
        fetch.start()
        fetch.wait()
        per_row = []
        for g in range(16):
            span = slice(16 * g, 16 * g + 16)
            left = full_ref[2 * g].astype(F32) * factor
            right = full_ref[2 * g + 1].astype(F32) * factor
            g_in[span, :512] = left
            g_in[span, 512:] = right[:, :256]
            g_out[span, :] = right[:, 256:]
            w = w_ref[span, :].astype(F32)
            term = jnp.sum(left * w[:, :512], axis=1, keepdims=True)
            per_row.append(term + jnp.sum(right[:, :256] * w[:, 512:], axis=1, keepdims=True))
        column = jnp.broadcast_to(jnp.concatenate(per_row, axis=0), (D, 128))
        g_gain[...] = jnp.transpose(column)[0:1] / gain_ref[...]
        copy.wait()

    vmem = pl.BlockSpec(memory_space=pltpu.VMEM)
    hbm = pl.BlockSpec(memory_space=pltpu.HBM)
    return pl.pallas_call(
        kernel,
        out_shape=(
            jax.ShapeDtypeStruct((OWN, COLS, D), BF16),
            jax.ShapeDtypeStruct((D, 3 * D), F32),
            jax.ShapeDtypeStruct((D, D), F32),
            jax.ShapeDtypeStruct((1, D), F32),
        ),
        in_specs=[hbm, hbm, vmem, vmem],
        out_specs=(hbm, vmem, vmem, vmem),
        scratch_shapes=[pltpu.VMEM((32, 16, 512), BF16), pltpu.SemaphoreType.DMA((2,))],
        compiler_params=pltpu.CompilerParams(vmem_limit_bytes=VMEM_BYTES),
    )(gt, full, gain, w_in)


def local(tokens, norm_gain, in_weight, out_weight, cotangent):
    factor = 1.0 / math.sqrt(lax.axis_size("rows") * lax.axis_size("dp") * OWN * COLS)
    gain = norm_gain.reshape(1, D)
    gt, full = block(tokens[0], cotangent[0], gain, in_weight, out_weight)
    gt, g_in, g_out, g_gain = outputs(gt, full, gain, in_weight, factor)
    return gt[None], g_in, g_out, g_gain.reshape(D)


def solution(mesh):
    return jax.shard_map(
        local,
        mesh=mesh,
        in_specs=(P("dp", "rows", None, None), P(), P(), P(), P("dp", "rows", None, None)),
        out_specs=(P("dp", "rows", None, None), P(), P(), P()),
        check_vma=False,
    )
```

```python
import math
from types import SimpleNamespace

import jax
import jax.numpy as jnp
from jax import lax
from jax.experimental import pallas as pl
from jax.experimental.pallas import tpu as pltpu
from jax.sharding import PartitionSpec as P

F32 = jnp.float32
BF16 = jnp.bfloat16
D = 256
COLS = 128
OWN = 16
FRAME = OWN + 6
PADDED = 144
NEG = -1e30
NT = (((1,), (1,)), ((), ()))
TN = (((0,), (0,)), ((), ()))
VMEM_BYTES = 58 * 1024 * 1024

BUFFERS = {
    "halo": ((2, 3, COLS, D), BF16),
    "shifted": ((2, PADDED, D), F32),
    "normed": ((FRAME, COLS, D), BF16),
    "k_win": ((FRAME, 16, 16, D), BF16),
    "v_win": ((FRAME, 16, 16, D), BF16),
    "q_tiles": ((2, 16, 64, D), BF16),
    "g_tiles": ((2, 16, 64, D), BF16),
    "attended": ((OWN, COLS, D), BF16),
    "joined": ((FRAME, COLS, 3 * D), BF16),
    "bias": ((2, 3, 224, D), F32),
    "acc": ((FRAME, PADDED, 2 * D), F32),
    "gn": ((OWN, COLS, D), F32),
    "sums": ((32, 16, 512), BF16),
    "rim_out": ((2, 3, COLS, D), BF16),
    "rim_in": ((2, 3, COLS, D), BF16),
}


def dot(a, b, dims=(((1,), (0,)), ((), ()))):
    return lax.dot_general(a, b, dims, preferred_element_type=F32)


def inverse_rms(wide):
    return lax.rsqrt(jnp.mean(wide * wide, axis=-1, keepdims=True) + 1e-6)


def windows(b, x, slot, frame_row):
    wide = x.astype(F32)
    normed = wide * inverse_rms(wide) * b.gain[...]
    b.normed[frame_row] = normed.astype(BF16)
    b.shifted[slot, 4 : 4 + COLS, :] = normed
    rows = jnp.concatenate([b.shifted[slot, 8 * j : 8 * j + 16, :] for j in range(16)], axis=0)
    kv = dot(rows.astype(BF16), b.w_in[:, D:])
    b.k_win[frame_row] = kv[:, :D].astype(BF16).reshape(16, 16, D)
    b.v_win[frame_row] = kv[:, D:].astype(BF16).reshape(16, 16, D)


def clear(b):
    b.shifted[...] = jnp.zeros_like(b.shifted)
    for r in range(3):
        b.joined[r, :, :D] = jnp.zeros((COLS, D), BF16)
        b.joined[OWN + 3 + r, :, :D] = jnp.zeros((COLS, D), BF16)

    def zero_row(r, carry):
        b.acc[r] = jnp.zeros((PADDED, 2 * D), F32)
        return carry

    lax.fori_loop(0, FRAME, zero_row, 0)


def mask(b, here, last):
    key = lax.broadcasted_iota(jnp.int32, (224, D), 0)
    lane = lax.broadcasted_iota(jnp.int32, (224, D), 1)
    k_row, k_col = key // 16, key % 16
    q_row, q_col = (lane % 64) // 8, lane % 8
    near = (k_row - q_row >= 0) & (k_row - q_row <= 6) & (k_col - q_col >= 1) & (k_col - q_col <= 7)
    for half in range(2):
        if half == 0:
            inside = near & ((k_row >= 3) | (here > 0))
        else:
            inside = near & ((k_row < 11) | (here < last))
        for side in range(3):
            ok = inside
            if side == 0:
                ok = ok & (k_col >= 4)
            if side == 2:
                ok = ok & (k_col < 12)
            b.bias[half, side] = jnp.where(ok, 0.0, NEG)


def own_rows(b):
    def tile_order(pair):
        return [
            jnp.concatenate([pair[8 * j : 8 * j + 8], pair[COLS + 8 * j : COLS + 8 * j + 8]], axis=0)
            for j in range(16)
        ]

    def own_pair(i, carry):
        first = 2 * i
        half = i // 4
        place = pl.multiple_of((i % 4) * 16, 16)
        windows(b, b.tok[first], 0, first + 3)
        windows(b, b.tok[first + 1], 1, first + 4)
        both = b.normed[pl.ds(first + 3, 2)].reshape(2 * COLS, D)
        q = dot(both, b.w_in[:, :D])
        for j, tile in enumerate(tile_order(q)):
            b.q_tiles[half, j, pl.ds(place, 16), :] = (tile.astype(BF16).astype(F32) * 0.125).astype(BF16)
        g = dot(b.cot[pl.ds(first, 2)].reshape(2 * COLS, D), b.w_out[...], NT)
        for j, tile in enumerate(tile_order(g)):
            b.g_tiles[half, j, pl.ds(place, 16), :] = tile.astype(BF16)
        return carry

    lax.fori_loop(0, 8, own_pair, 0)


def halo_rows(b):
    def halo_row(r, carry):
        windows(b, b.halo[0, r], 0, r)
        windows(b, b.halo[1, r], 1, OWN + 3 + r)
        return carry

    lax.fori_loop(0, 3, halo_row, 0)


def attend(b):
    head_lane = lax.broadcasted_iota(jnp.int32, (64, D), 1) // 64

    def by_head(tile):
        return jnp.concatenate(
            [jnp.where(head_lane == h, tile, jnp.zeros_like(tile)) for h in range(4)], axis=0
        )

    def of_heads(full):
        out = full[192:256]
        for h in (2, 1, 0):
            out = jnp.where(head_lane == h, full[64 * h : 64 * h + 64], out)
        return out

    def one_tile(half, j, side):
        frame = half * 8
        k = b.k_win[pl.ds(frame, 14), j].reshape(224, D)
        v = b.v_win[pl.ds(frame, 14), j].reshape(224, D)
        q = by_head(b.q_tiles[half, j])
        g = by_head(b.g_tiles[half, j])
        s = dot(k, q, NT) + b.bias[half, side]
        e = jnp.exp(s - jnp.max(s, axis=0, keepdims=True))
        p = e * (1.0 / jnp.sum(e, axis=0, keepdims=True))
        weights = p.astype(BF16)
        dp = dot(v, g, NT)
        delta = jnp.sum(p * dp, axis=0, keepdims=True)
        ds = (p * (dp - delta)).astype(BF16)
        place = pl.ds(pl.multiple_of(8 * j, 8), 16)
        b.acc[pl.ds(frame, 14), place, :D] += dot(ds, q).reshape(14, 16, D)
        b.acc[pl.ds(frame, 14), place, D:] += dot(weights, g).reshape(14, 16, D)
        att = of_heads(dot(weights, v, TN))
        dq = of_heads(dot(ds, k, TN)) * 0.125
        return att.reshape(8, 8, D), dq.reshape(8, 8, D)

    def tile_pair(i, carry):
        one_pair(0, i)
        one_pair(1, i)
        return carry

    def one_pair(half, jp):
        a0, d0 = one_tile(half, 2 * jp, jnp.where(jp == 0, 0, 1))
        a1, d1 = one_tile(half, 2 * jp + 1, jnp.where(jp == 7, 2, 1))
        cols = pl.ds(pl.multiple_of(16 * jp, 16), 16)
        b.attended[pl.ds(half * 8, 8), cols, :] = jnp.concatenate([a0, a1], axis=1).astype(BF16)
        b.joined[pl.ds(half * 8 + 3, 8), cols, :D] = jnp.concatenate([d0, d1], axis=1).astype(BF16)

    lax.fori_loop(0, 8, tile_pair, 0)


def weight_sums(b):
    def key_row(r, carry):
        b.joined[r, :, D:] = b.acc[r, 4 : 4 + COLS, :].astype(BF16)
        return carry

    lax.fori_loop(0, FRAME, key_row, 0)
    g_in = dot(b.normed[...].reshape(FRAME * COLS, D), b.joined[...].reshape(FRAME * COLS, 3 * D), TN)
    g_out = dot(b.attended[...].reshape(OWN * COLS, D), b.cot[...].reshape(OWN * COLS, D), TN)
    for g in range(16):
        span = slice(16 * g, 16 * g + 16)
        b.sums[2 * g] = g_in[span, :512].astype(BF16)
        b.sums[2 * g + 1] = jnp.concatenate([g_in[span, 512:], g_out[span]], axis=1).astype(BF16)


def rim_rows(b):
    for side, first in ((0, 0), (1, OWN + 3)):
        rows = b.joined[first : first + 3].reshape(3 * COLS, 3 * D)
        b.rim_out[side] = dot(rows, b.w_in[...], NT).reshape(3, COLS, D).astype(BF16)


def own_gn(b):
    def four(i, carry):
        rows = b.joined[pl.ds(3 + 4 * i, 4)].reshape(4 * COLS, 3 * D)
        b.gn[pl.ds(4 * i, 4)] = dot(rows, b.w_in[...], NT).reshape(4, COLS, D)
        return carry

    lax.fori_loop(0, 4, four, 0)


def finish(b, row, rim=None):
    wide = b.tok[row].astype(F32)
    inv = inverse_rms(wide)
    gn = b.gn[row]
    if rim is not None:
        gn = gn + rim.astype(F32)
    gained = gn * b.gain[...]
    mean = jnp.mean(gained * wide, axis=-1, keepdims=True)
    b.gt[row] = (inv * (gained - wide * (inv * inv * mean))).astype(BF16)


def finish_rows(b, low, high):
    def body(r, carry):
        finish(b, r)
        return carry

    lax.fori_loop(low, high, body, 0)


def block_kernel(names, *refs):
    b = SimpleNamespace(**dict(zip(names, refs)))
    rows = lax.axis_index("rows")
    count = lax.axis_size("rows")
    x = lax.axis_index("dp")
    core = rows % 2
    z = (rows // 2) % 8
    y = rows // 16
    me = y * 4 + x
    before = {"rows": (rows + count - 1) % count, "dp": x}
    after = {"rows": (rows + 1) % count, "dp": x}
    partner = {"rows": rows + 1 - 2 * core, "dp": x}
    mine = 16 * core
    other = 16 - mine

    def in_plane(i):
        to_y, to_x = (y + i // 4) % 4, (x + i % 4) % 4
        return {"rows": (to_y * 8 + z) * 2 + core, "dp": to_x}, to_y * 4 + to_x

    def from_plane(i):
        return ((y + 4 - i // 4) % 4) * 4 + (x + 4 - i % 4) % 4

    def along_z(i):
        return {"rows": (y * 8 + (z + i) % 8) * 2 + core, "dp": x}

    def remote(src, dst, send, recv, where):
        return pltpu.make_async_remote_copy(
            src_ref=src, dst_ref=dst, send_sem=send, recv_sem=recv,
            device_id=where, device_id_type=pl.DeviceIdType.MESH,
        )

    barrier = pltpu.get_barrier_semaphore()

    def greet(where):
        pl.semaphore_signal(barrier, inc=1, device_id=where, device_id_type=pl.DeviceIdType.MESH)

    def greet_plane(i, carry):
        greet(in_plane(i)[0])
        return carry

    def greet_z(i, carry):
        greet(along_z(i))
        return carry

    greet(before)
    greet(after)
    greet(partner)
    lax.fori_loop(1, 16, greet_plane, 0)
    lax.fori_loop(1, 8, greet_z, 0)
    clear(b)
    pl.semaphore_wait(barrier, 25)

    def halo_copies():
        return (
            remote(b.tok.at[pl.ds(OWN - 3, 3)], b.halo.at[0], b.near_send.at[0], b.near_recv.at[0], after),
            remote(b.tok.at[pl.ds(0, 3)], b.halo.at[1], b.near_send.at[1], b.near_recv.at[1], before),
        )

    def rim_copies():
        return (
            remote(b.rim_out.at[0], b.rim_in.at[1], b.near_send.at[2], b.near_recv.at[2], before),
            remote(b.rim_out.at[1], b.rim_in.at[0], b.near_send.at[3], b.near_recv.at[3], after),
        )

    def core_scatter(i):
        place = in_plane(i)[1]
        return remote(b.sums.at[other + place], b.core_got.at[i], b.core_send.at[i], b.core_recv.at[i], partner)

    def scatter(i):
        where, place = in_plane(i)
        return remote(b.paired.at[i], b.plane_got.at[i], b.plane_send.at[i], b.plane_recv.at[i], where)

    def z_share(i):
        where = along_z(i)
        return remote(b.z_all.at[z], b.z_all.at[z], b.z_send.at[i], b.z_recv.at[i], where)

    def gather(i):
        where, place = in_plane(i)
        return remote(b.full.at[mine + me], b.full.at[mine + me], b.out_send.at[i], b.out_recv.at[i], where)

    def core_gather(i):
        chunk = b.full.at[mine + from_plane(i)]
        return remote(chunk, chunk, b.last_send.at[i], b.last_recv.at[i], partner)

    def each(make, low, high, act):
        def body(i, carry):
            act(make(i))
            return carry

        lax.fori_loop(low, high, body, 0)

    def start(copy):
        copy.start()

    def wait_send(copy):
        copy.wait_send()

    def wait_recv(copy):
        copy.wait_recv()

    for copy in halo_copies():
        copy.start()
    mask(b, rows, count - 1)
    own_rows(b)
    for copy in halo_copies():
        copy.wait_recv()
    halo_rows(b)
    attend(b)
    weight_sums(b)
    each(core_scatter, 1, 16, start)
    core_scatter(0).start()
    rim_rows(b)
    for copy in rim_copies():
        copy.start()

    def pair(i):
        core_scatter(i).wait_recv()
        return b.sums[mine + in_plane(i)[1]].astype(F32) + b.core_got[i].astype(F32)

    def pair_and_send(i, carry):
        b.paired[i] = pair(i).astype(BF16)
        scatter(i).start()
        return carry

    lax.fori_loop(1, 16, pair_and_send, 0)
    own_gn(b)

    def add_plane(i, total):
        scatter(i).wait_recv()
        return total + b.plane_got[i].astype(F32)

    total = lax.fori_loop(1, 16, add_plane, pair(0))
    b.z_all[z] = total.astype(BF16)
    each(z_share, 1, 8, start)
    finish_rows(b, 3, 13)
    each(z_share, 1, 8, wait_recv)
    whole = b.z_all[0].astype(F32)
    for i in range(1, 8):
        whole = whole + b.z_all[i].astype(F32)
    b.full[mine + me] = whole.astype(BF16)
    each(gather, 1, 16, start)
    core_gather(0).start()
    for copy in rim_copies():
        copy.wait_recv()

    def edge(r, carry):
        finish(b, r, b.rim_in[0, r])
        finish(b, OWN - 3 + r, b.rim_in[1, r])
        return carry

    lax.fori_loop(0, 3, edge, 0)

    def pass_on(i, carry):
        gather(i).wait_recv()
        core_gather(i).start()
        return carry

    lax.fori_loop(1, 16, pass_on, 0)
    each(core_gather, 0, 16, wait_recv)
    for copy in halo_copies() + rim_copies():
        copy.wait_send()
    each(core_scatter, 0, 16, wait_send)
    each(scatter, 1, 16, wait_send)
    each(z_share, 1, 8, wait_send)
    each(gather, 1, 16, wait_send)
    each(core_gather, 0, 16, wait_send)


def block(tok, cot, gain, w_in, w_out):
    vmem = pl.BlockSpec(memory_space=pltpu.VMEM)
    dma = pltpu.SemaphoreType.DMA
    outs = {"gt": ((OWN, COLS, D), BF16), "full": ((32, 16, 512), BF16)}
    slots = {
        "core_got": ((16, 16, 512), BF16),
        "paired": ((16, 16, 512), BF16),
        "plane_got": ((16, 16, 512), BF16),
        "z_all": ((8, 16, 512), BF16),
    }
    sems = {
        "near_send": 4, "near_recv": 4, "core_send": 16, "core_recv": 16, "plane_send": 16, "plane_recv": 16,
        "z_send": 8, "z_recv": 8, "out_send": 16, "out_recv": 16,
        "last_send": 16, "last_recv": 16,
    }
    names = ["tok", "cot", "gain", "w_in", "w_out", *outs, *BUFFERS, *slots, *sems]

    def kernel(*refs):
        block_kernel(names, *refs)

    return pl.pallas_call(
        kernel,
        out_shape=tuple(jax.ShapeDtypeStruct(*o) for o in outs.values()),
        in_specs=[vmem] * 5,
        out_specs=(vmem,) * 2,
        scratch_shapes=[
            *(pltpu.VMEM(*s) for s in BUFFERS.values()),
            *(pltpu.VMEM(*s) for s in slots.values()),
            *(dma((n,)) for n in sems.values()),
        ],
        compiler_params=pltpu.CompilerParams(
            collective_id=0, has_side_effects=True, vmem_limit_bytes=VMEM_BYTES
        ),
    )(tok, cot, gain, w_in, w_out)


def outputs(gt, full, gain, w_in, factor):
    def kernel(gt_hbm, full_hbm, gain_hbm, w_hbm, gt_out, g_in_out, g_out_out, g_gain_out,
               rows, full_ref, gain_ref, w, g_in, g_out, g_gain, sem):
        quarters = [pl.ds(4 * i, 4) for i in range(4)]
        spans = [pl.ds(64 * i, 64) for i in range(4)]

        def copies(first, pairs):
            return [pltpu.make_async_copy(src, dst, sem.at[first + i]) for i, (src, dst) in enumerate(pairs)]

        parts = copies(0, [(full_hbm.at[pl.ds(8 * i, 8)], full_ref.at[pl.ds(8 * i, 8)]) for i in range(4)])
        small = copies(4, [(w_hbm, w), (gain_hbm, gain_ref)])
        reads = copies(6, [(gt_hbm.at[r], rows.at[r]) for r in quarters])
        writes = copies(10, [(rows.at[r], gt_out.at[r]) for r in quarters])
        in_writes = copies(14, [(g_in.at[r], g_in_out.at[r]) for r in spans])
        out_writes = copies(18, [(g_out.at[r], g_out_out.at[r]) for r in spans])
        gain_write = pltpu.make_async_copy(g_gain, g_gain_out, sem.at[22])
        for copy in parts + small + reads:
            copy.start()
        for i in range(4):
            parts[i].wait()
            for g in range(4 * i, 4 * i + 4):
                span = slice(16 * g, 16 * g + 16)
                right = full_ref[2 * g + 1].astype(F32) * factor
                g_in[span, :512] = full_ref[2 * g].astype(F32) * factor
                g_in[span, 512:] = right[:, :256]
                g_out[span, :] = right[:, 256:]
            in_writes[i].start()
            out_writes[i].start()
            reads[i].wait()
            writes[i].start()
        for copy in small:
            copy.wait()
        per_row = jnp.sum(g_in[...] * w[...].astype(F32), axis=1, keepdims=True)
        g_gain[...] = jnp.transpose(jnp.broadcast_to(per_row, (D, 128)))[0:1] / gain_ref[...]
        gain_write.start()
        for copy in writes + in_writes + out_writes + [gain_write]:
            copy.wait()

    hbm = pl.BlockSpec(memory_space=pltpu.HBM)
    return pl.pallas_call(
        kernel,
        out_shape=(
            jax.ShapeDtypeStruct((OWN, COLS, D), BF16),
            jax.ShapeDtypeStruct((D, 3 * D), F32),
            jax.ShapeDtypeStruct((D, D), F32),
            jax.ShapeDtypeStruct((1, D), F32),
        ),
        in_specs=[hbm] * 4,
        out_specs=(hbm,) * 4,
        scratch_shapes=[
            pltpu.VMEM((OWN, COLS, D), BF16),
            pltpu.VMEM((32, 16, 512), BF16),
            pltpu.VMEM((1, D), F32),
            pltpu.VMEM((D, 3 * D), BF16),
            pltpu.VMEM((D, 3 * D), F32),
            pltpu.VMEM((D, D), F32),
            pltpu.VMEM((1, D), F32),
            pltpu.SemaphoreType.DMA((23,)),
        ],
        compiler_params=pltpu.CompilerParams(vmem_limit_bytes=VMEM_BYTES),
    )(gt, full, gain, w_in)


def local(tokens, norm_gain, in_weight, out_weight, cotangent):
    factor = 1.0 / math.sqrt(lax.axis_size("rows") * lax.axis_size("dp") * OWN * COLS)
    gain = norm_gain.reshape(1, D)
    gt, full = block(tokens[0], cotangent[0], gain, in_weight, out_weight)
    gt, g_in, g_out, g_gain = outputs(gt, full, gain, in_weight, factor)
    return gt[None], g_in, g_out, g_gain.reshape(D)


def solution(mesh):
    return jax.shard_map(
        local,
        mesh=mesh,
        in_specs=(P("dp", "rows", None, None), P(), P(), P(), P("dp", "rows", None, None)),
        out_specs=(P("dp", "rows", None, None), P(), P(), P()),
        check_vma=False,
    )
```

```python
import math
from types import SimpleNamespace

import jax
import jax.numpy as jnp
from jax import lax
from jax.experimental import pallas as pl
from jax.experimental.pallas import tpu as pltpu
from jax.sharding import PartitionSpec as P

F32 = jnp.float32
BF16 = jnp.bfloat16
D = 256
COLS = 128
OWN = 16
FRAME = OWN + 6
PADDED = 144
NEG = -1e30
NT = (((1,), (1,)), ((), ()))
TN = (((0,), (0,)), ((), ()))
VMEM_BYTES = 58 * 1024 * 1024

BUFFERS = {
    "halo": ((2, 3, COLS, D), BF16),
    "shifted": ((2, PADDED, D), F32),
    "normed": ((FRAME, COLS, D), BF16),
    "k_win": ((FRAME, 16, 16, D), BF16),
    "v_win": ((FRAME, 16, 16, D), BF16),
    "q_tiles": ((2, 16, 64, D), BF16),
    "g_tiles": ((2, 16, 64, D), BF16),
    "attended": ((OWN, COLS, D), BF16),
    "joined": ((FRAME, COLS, 3 * D), BF16),
    "bias": ((2, 3, 224, D), F32),
    "acc": ((FRAME, PADDED, 2 * D), F32),
    "gn": ((OWN, COLS, D), F32),
    "sums": ((32, 16, 512), BF16),
    "rim_out": ((2, 3, COLS, D), BF16),
    "rim_in": ((2, 3, COLS, D), BF16),
}


def dot(a, b, dims=(((1,), (0,)), ((), ()))):
    return lax.dot_general(a, b, dims, preferred_element_type=F32)


def inverse_rms(wide):
    return lax.rsqrt(jnp.mean(wide * wide, axis=-1, keepdims=True) + 1e-6)


def windows(b, x, slot, frame_row):
    wide = x.astype(F32)
    normed = wide * inverse_rms(wide) * b.gain[...]
    b.normed[frame_row] = normed.astype(BF16)
    b.shifted[slot, 4 : 4 + COLS, :] = normed
    rows = jnp.concatenate([b.shifted[slot, 8 * j : 8 * j + 16, :] for j in range(16)], axis=0)
    kv = dot(rows.astype(BF16), b.w_in[:, D:])
    b.k_win[frame_row] = kv[:, :D].astype(BF16).reshape(16, 16, D)
    b.v_win[frame_row] = kv[:, D:].astype(BF16).reshape(16, 16, D)


def clear(b):
    b.shifted[...] = jnp.zeros_like(b.shifted)
    for r in range(3):
        b.joined[r, :, :D] = jnp.zeros((COLS, D), BF16)
        b.joined[OWN + 3 + r, :, :D] = jnp.zeros((COLS, D), BF16)

    def zero_row(r, carry):
        b.acc[r] = jnp.zeros((PADDED, 2 * D), F32)
        return carry

    lax.fori_loop(0, FRAME, zero_row, 0)


def mask(b, here, last):
    key = lax.broadcasted_iota(jnp.int32, (224, D), 0)
    lane = lax.broadcasted_iota(jnp.int32, (224, D), 1)
    k_row, k_col = key // 16, key % 16
    q_row, q_col = (lane % 64) // 8, lane % 8
    near = (k_row - q_row >= 0) & (k_row - q_row <= 6) & (k_col - q_col >= 1) & (k_col - q_col <= 7)
    for half in range(2):
        if half == 0:
            inside = near & ((k_row >= 3) | (here > 0))
        else:
            inside = near & ((k_row < 11) | (here < last))
        for side in range(3):
            ok = inside
            if side == 0:
                ok = ok & (k_col >= 4)
            if side == 2:
                ok = ok & (k_col < 12)
            b.bias[half, side] = jnp.where(ok, 0.0, NEG)


def own_rows(b):
    def tile_order(pair):
        return [
            jnp.concatenate([pair[8 * j : 8 * j + 8], pair[COLS + 8 * j : COLS + 8 * j + 8]], axis=0)
            for j in range(16)
        ]

    def own_pair(i, carry):
        first = 2 * i
        half = i // 4
        place = pl.multiple_of((i % 4) * 16, 16)
        windows(b, b.tok[first], 0, first + 3)
        windows(b, b.tok[first + 1], 1, first + 4)
        both = b.normed[pl.ds(first + 3, 2)].reshape(2 * COLS, D)
        q = dot(both, b.w_in[:, :D])
        for j, tile in enumerate(tile_order(q)):
            b.q_tiles[half, j, pl.ds(place, 16), :] = (tile.astype(BF16).astype(F32) * 0.125).astype(BF16)
        g = dot(b.cot[pl.ds(first, 2)].reshape(2 * COLS, D), b.w_out[...], NT)
        for j, tile in enumerate(tile_order(g)):
            b.g_tiles[half, j, pl.ds(place, 16), :] = tile.astype(BF16)
        return carry

    lax.fori_loop(0, 8, own_pair, 0)


def halo_rows(b):
    def halo_row(r, carry):
        windows(b, b.halo[0, r], 0, r)
        windows(b, b.halo[1, r], 1, OWN + 3 + r)
        return carry

    lax.fori_loop(0, 3, halo_row, 0)


def attend(b):
    head_lane = lax.broadcasted_iota(jnp.int32, (64, D), 1) // 64

    def by_head(tile):
        return jnp.concatenate(
            [jnp.where(head_lane == h, tile, jnp.zeros_like(tile)) for h in range(4)], axis=0
        )

    def of_heads(full):
        out = full[192:256]
        for h in (2, 1, 0):
            out = jnp.where(head_lane == h, full[64 * h : 64 * h + 64], out)
        return out

    def some_tiles(tiles):
        n = range(len(tiles))
        k = [b.k_win[pl.ds(half * 8, 14), j].reshape(224, D) for half, j, side in tiles]
        v = [b.v_win[pl.ds(half * 8, 14), j].reshape(224, D) for half, j, side in tiles]
        q = [by_head(b.q_tiles[half, j]) for half, j, side in tiles]
        g = [by_head(b.g_tiles[half, j]) for half, j, side in tiles]
        s = [dot(k[i], q[i], NT) + b.bias[half, side] for i, (half, j, side) in enumerate(tiles)]
        dp = [dot(v[i], g[i], NT) for i in n]
        e = [jnp.exp(s[i] - jnp.max(s[i], axis=0, keepdims=True)) for i in n]
        p = [e[i] * (1.0 / jnp.sum(e[i], axis=0, keepdims=True)) for i in n]
        weights = [p[i].astype(BF16) for i in n]
        for i, (half, j, side) in enumerate(tiles):
            b.acc[pl.ds(half * 8, 14), pl.ds(pl.multiple_of(8 * j, 8), 16), D:] += dot(weights[i], g[i]).reshape(14, 16, D)
        att = [of_heads(dot(weights[i], v[i], TN)).reshape(8, 8, D) for i in n]
        delta = [jnp.sum(p[i] * dp[i], axis=0, keepdims=True) for i in n]
        ds = [(p[i] * (dp[i] - delta[i])).astype(BF16) for i in n]
        for i, (half, j, side) in enumerate(tiles):
            b.acc[pl.ds(half * 8, 14), pl.ds(pl.multiple_of(8 * j, 8), 16), :D] += dot(ds[i], q[i]).reshape(14, 16, D)
        dq = [(of_heads(dot(ds[i], k[i], TN)) * 0.125).reshape(8, 8, D) for i in n]
        return att, dq

    def store(half, jp, att, dq):
        cols = pl.ds(pl.multiple_of(16 * jp, 16), 16)
        b.attended[pl.ds(half * 8, 8), cols, :] = jnp.concatenate(att, axis=1).astype(BF16)
        b.joined[pl.ds(half * 8 + 3, 8), cols, :D] = jnp.concatenate(dq, axis=1).astype(BF16)

    def tile_pairs(jp, carry):
        left, right = jnp.where(jp == 0, 0, 1), jnp.where(jp == 7, 2, 1)
        att, dq = some_tiles([(half, 2 * jp + i, (left, right)[i]) for half in range(2) for i in range(2)])
        for half in range(2):
            store(half, jp, att[2 * half : 2 * half + 2], dq[2 * half : 2 * half + 2])
        return carry

    lax.fori_loop(0, 8, tile_pairs, 0)


def weight_sums(b):
    def key_row(r, carry):
        b.joined[r, :, D:] = b.acc[r, 4 : 4 + COLS, :].astype(BF16)
        return carry

    lax.fori_loop(0, FRAME, key_row, 0)
    g_in = dot(b.normed[...].reshape(FRAME * COLS, D), b.joined[...].reshape(FRAME * COLS, 3 * D), TN)
    g_out = dot(b.attended[...].reshape(OWN * COLS, D), b.cot[...].reshape(OWN * COLS, D), TN)
    for g in range(16):
        span = slice(16 * g, 16 * g + 16)
        b.sums[2 * g] = g_in[span, :512].astype(BF16)
        b.sums[2 * g + 1] = jnp.concatenate([g_in[span, 512:], g_out[span]], axis=1).astype(BF16)


def rim_rows(b):
    for side, first in ((0, 0), (1, OWN + 3)):
        rows = b.joined[first : first + 3].reshape(3 * COLS, 3 * D)
        b.rim_out[side] = dot(rows, b.w_in[...], NT).reshape(3, COLS, D).astype(BF16)


def own_gn(b):
    def four(i, carry):
        rows = b.joined[pl.ds(3 + 4 * i, 4)].reshape(4 * COLS, 3 * D)
        b.gn[pl.ds(4 * i, 4)] = dot(rows, b.w_in[...], NT).reshape(4, COLS, D)
        return carry

    lax.fori_loop(0, 4, four, 0)


def finish(b, row, rim=None):
    wide = b.tok[row].astype(F32)
    inv = inverse_rms(wide)
    gn = b.gn[row]
    if rim is not None:
        gn = gn + rim.astype(F32)
    gained = gn * b.gain[...]
    mean = jnp.mean(gained * wide, axis=-1, keepdims=True)
    b.gt[row] = (inv * (gained - wide * (inv * inv * mean))).astype(BF16)


def finish_rows(b, low, high):
    def body(r, carry):
        finish(b, r)
        return carry

    lax.fori_loop(low, high, body, 0)


def block_kernel(names, *refs):
    b = SimpleNamespace(**dict(zip(names, refs)))
    rows = lax.axis_index("rows")
    count = lax.axis_size("rows")
    x = lax.axis_index("dp")
    core = rows % 2
    z = (rows // 2) % 8
    y = rows // 16
    me = y * 4 + x
    before = {"rows": (rows + count - 1) % count, "dp": x}
    after = {"rows": (rows + 1) % count, "dp": x}
    partner = {"rows": rows + 1 - 2 * core, "dp": x}
    mine = 16 * core
    other = 16 - mine

    def in_plane(i):
        to_y, to_x = (y + i // 4) % 4, (x + i % 4) % 4
        return {"rows": (to_y * 8 + z) * 2 + core, "dp": to_x}, to_y * 4 + to_x

    def from_plane(i):
        return ((y + 4 - i // 4) % 4) * 4 + (x + 4 - i % 4) % 4

    def along_z(i):
        return {"rows": (y * 8 + (z + i) % 8) * 2 + core, "dp": x}

    def remote(src, dst, send, recv, where):
        return pltpu.make_async_remote_copy(
            src_ref=src, dst_ref=dst, send_sem=send, recv_sem=recv,
            device_id=where, device_id_type=pl.DeviceIdType.MESH,
        )

    barrier = pltpu.get_barrier_semaphore()

    def greet(where):
        pl.semaphore_signal(barrier, inc=1, device_id=where, device_id_type=pl.DeviceIdType.MESH)

    def greet_plane(i, carry):
        greet(in_plane(i)[0])
        return carry

    def greet_z(i, carry):
        greet(along_z(i))
        return carry

    greet(before)
    greet(after)
    greet(partner)
    lax.fori_loop(1, 16, greet_plane, 0)
    lax.fori_loop(1, 8, greet_z, 0)
    clear(b)
    pl.semaphore_wait(barrier, 25)

    def halo_copies():
        return (
            remote(b.tok.at[pl.ds(OWN - 3, 3)], b.halo.at[0], b.near_send.at[0], b.near_recv.at[0], after),
            remote(b.tok.at[pl.ds(0, 3)], b.halo.at[1], b.near_send.at[1], b.near_recv.at[1], before),
        )

    def rim_copies():
        return (
            remote(b.rim_out.at[0], b.rim_in.at[1], b.near_send.at[2], b.near_recv.at[2], before),
            remote(b.rim_out.at[1], b.rim_in.at[0], b.near_send.at[3], b.near_recv.at[3], after),
        )

    def core_scatter(i):
        place = in_plane(i)[1]
        return remote(b.sums.at[other + place], b.core_got.at[i], b.core_send.at[i], b.core_recv.at[i], partner)

    def scatter(i):
        where, place = in_plane(i)
        return remote(b.paired.at[i], b.plane_got.at[i], b.plane_send.at[i], b.plane_recv.at[i], where)

    def z_share(i):
        where = along_z(i)
        return remote(b.z_all.at[z], b.z_all.at[z], b.z_send.at[i], b.z_recv.at[i], where)

    def gather(i):
        where, place = in_plane(i)
        return remote(b.full.at[mine + me], b.full.at[mine + me], b.out_send.at[i], b.out_recv.at[i], where)

    def core_gather(i):
        chunk = b.full.at[mine + from_plane(i)]
        return remote(chunk, chunk, b.last_send.at[i], b.last_recv.at[i], partner)

    def each(make, low, high, act):
        def body(i, carry):
            act(make(i))
            return carry

        lax.fori_loop(low, high, body, 0)

    def start(copy):
        copy.start()

    def wait_send(copy):
        copy.wait_send()

    def wait_recv(copy):
        copy.wait_recv()

    for copy in halo_copies():
        copy.start()
    mask(b, rows, count - 1)
    own_rows(b)
    for copy in halo_copies():
        copy.wait_recv()
    halo_rows(b)
    attend(b)
    weight_sums(b)
    each(core_scatter, 1, 16, start)
    core_scatter(0).start()
    rim_rows(b)
    for copy in rim_copies():
        copy.start()

    def pair(i):
        core_scatter(i).wait_recv()
        return b.sums[mine + in_plane(i)[1]].astype(F32) + b.core_got[i].astype(F32)

    def pair_and_send(i, carry):
        b.paired[i] = pair(i).astype(BF16)
        scatter(i).start()
        return carry

    lax.fori_loop(1, 16, pair_and_send, 0)
    own_gn(b)

    def add_plane(i, total):
        scatter(i).wait_recv()
        return total + b.plane_got[i].astype(F32)

    total = lax.fori_loop(1, 16, add_plane, pair(0))
    b.z_all[z] = total.astype(BF16)
    each(z_share, 1, 8, start)
    finish_rows(b, 3, 13)
    each(z_share, 1, 8, wait_recv)
    whole = b.z_all[0].astype(F32)
    for i in range(1, 8):
        whole = whole + b.z_all[i].astype(F32)
    b.full[mine + me] = whole.astype(BF16)
    each(gather, 1, 16, start)
    core_gather(0).start()
    for copy in rim_copies():
        copy.wait_recv()

    def edge(r, carry):
        finish(b, r, b.rim_in[0, r])
        finish(b, OWN - 3 + r, b.rim_in[1, r])
        return carry

    lax.fori_loop(0, 3, edge, 0)

    def pass_on(i, carry):
        gather(i).wait_recv()
        core_gather(i).start()
        return carry

    lax.fori_loop(1, 16, pass_on, 0)
    each(core_gather, 0, 16, wait_recv)
    for copy in halo_copies() + rim_copies():
        copy.wait_send()
    each(core_scatter, 0, 16, wait_send)
    each(scatter, 1, 16, wait_send)
    each(z_share, 1, 8, wait_send)
    each(gather, 1, 16, wait_send)
    each(core_gather, 0, 16, wait_send)


def block(tok, cot, gain, w_in, w_out):
    vmem = pl.BlockSpec(memory_space=pltpu.VMEM)
    dma = pltpu.SemaphoreType.DMA
    outs = {"gt": ((OWN, COLS, D), BF16), "full": ((32, 16, 512), BF16)}
    slots = {
        "core_got": ((16, 16, 512), BF16),
        "paired": ((16, 16, 512), BF16),
        "plane_got": ((16, 16, 512), BF16),
        "z_all": ((8, 16, 512), BF16),
    }
    sems = {
        "near_send": 4, "near_recv": 4, "core_send": 16, "core_recv": 16, "plane_send": 16, "plane_recv": 16,
        "z_send": 8, "z_recv": 8, "out_send": 16, "out_recv": 16,
        "last_send": 16, "last_recv": 16,
    }
    names = ["tok", "cot", "gain", "w_in", "w_out", *outs, *BUFFERS, *slots, *sems]

    def kernel(*refs):
        block_kernel(names, *refs)

    return pl.pallas_call(
        kernel,
        out_shape=tuple(jax.ShapeDtypeStruct(*o) for o in outs.values()),
        in_specs=[vmem] * 5,
        out_specs=(vmem,) * 2,
        scratch_shapes=[
            *(pltpu.VMEM(*s) for s in BUFFERS.values()),
            *(pltpu.VMEM(*s) for s in slots.values()),
            *(dma((n,)) for n in sems.values()),
        ],
        compiler_params=pltpu.CompilerParams(
            collective_id=0, has_side_effects=True, vmem_limit_bytes=VMEM_BYTES
        ),
    )(tok, cot, gain, w_in, w_out)


def outputs(gt, full, gain, w_in, factor):
    def kernel(gt_hbm, full_hbm, gain_hbm, w_hbm, gt_out, g_in_out, g_out_out, g_gain_out,
               rows, full_ref, gain_ref, w, g_in, g_out, g_gain, sem):
        quarters = [pl.ds(4 * i, 4) for i in range(4)]
        spans = [pl.ds(64 * i, 64) for i in range(4)]

        def copies(first, pairs):
            return [pltpu.make_async_copy(src, dst, sem.at[first + i]) for i, (src, dst) in enumerate(pairs)]

        parts = copies(0, [(full_hbm.at[pl.ds(8 * i, 8)], full_ref.at[pl.ds(8 * i, 8)]) for i in range(4)])
        small = copies(4, [(w_hbm, w), (gain_hbm, gain_ref)])
        reads = copies(6, [(gt_hbm.at[r], rows.at[r]) for r in quarters])
        writes = copies(10, [(rows.at[r], gt_out.at[r]) for r in quarters])
        in_writes = copies(14, [(g_in.at[r], g_in_out.at[r]) for r in spans])
        out_writes = copies(18, [(g_out.at[r], g_out_out.at[r]) for r in spans])
        gain_write = pltpu.make_async_copy(g_gain, g_gain_out, sem.at[22])
        for copy in parts + small + reads:
            copy.start()
        for i in range(4):
            parts[i].wait()
            for g in range(4 * i, 4 * i + 4):
                span = slice(16 * g, 16 * g + 16)
                right = full_ref[2 * g + 1].astype(F32) * factor
                g_in[span, :512] = full_ref[2 * g].astype(F32) * factor
                g_in[span, 512:] = right[:, :256]
                g_out[span, :] = right[:, 256:]
            in_writes[i].start()
            out_writes[i].start()
            reads[i].wait()
            writes[i].start()
        for copy in small:
            copy.wait()
        per_row = jnp.sum(g_in[...] * w[...].astype(F32), axis=1, keepdims=True)
        g_gain[...] = jnp.transpose(jnp.broadcast_to(per_row, (D, 128)))[0:1] / gain_ref[...]
        gain_write.start()
        for copy in writes + in_writes + out_writes + [gain_write]:
            copy.wait()

    hbm = pl.BlockSpec(memory_space=pltpu.HBM)
    return pl.pallas_call(
        kernel,
        out_shape=(
            jax.ShapeDtypeStruct((OWN, COLS, D), BF16),
            jax.ShapeDtypeStruct((D, 3 * D), F32),
            jax.ShapeDtypeStruct((D, D), F32),
            jax.ShapeDtypeStruct((1, D), F32),
        ),
        in_specs=[hbm] * 4,
        out_specs=(hbm,) * 4,
        scratch_shapes=[
            pltpu.VMEM((OWN, COLS, D), BF16),
            pltpu.VMEM((32, 16, 512), BF16),
            pltpu.VMEM((1, D), F32),
            pltpu.VMEM((D, 3 * D), BF16),
            pltpu.VMEM((D, 3 * D), F32),
            pltpu.VMEM((D, D), F32),
            pltpu.VMEM((1, D), F32),
            pltpu.SemaphoreType.DMA((23,)),
        ],
        compiler_params=pltpu.CompilerParams(vmem_limit_bytes=VMEM_BYTES),
    )(gt, full, gain, w_in)


def local(tokens, norm_gain, in_weight, out_weight, cotangent):
    factor = 1.0 / math.sqrt(lax.axis_size("rows") * lax.axis_size("dp") * OWN * COLS)
    gain = norm_gain.reshape(1, D)
    gt, full = block(tokens[0], cotangent[0], gain, in_weight, out_weight)
    gt, g_in, g_out, g_gain = outputs(gt, full, gain, in_weight, factor)
    return gt[None], g_in, g_out, g_gain.reshape(D)


def solution(mesh):
    return jax.shard_map(
        local,
        mesh=mesh,
        in_specs=(P("dp", "rows", None, None), P(), P(), P(), P("dp", "rows", None, None)),
        out_specs=(P("dp", "rows", None, None), P(), P(), P()),
        check_vma=False,
    )
```

```python
import math
from types import SimpleNamespace

import jax
import jax.numpy as jnp
from jax import lax
from jax.experimental import pallas as pl
from jax.experimental.pallas import tpu as pltpu
from jax.sharding import PartitionSpec as P

F32 = jnp.float32
BF16 = jnp.bfloat16
D = 256
COLS = 128
OWN = 16
FRAME = OWN + 6
PADDED = 144
NEG = -1e30
KEYS = 160
LANES = 128
NT = (((1,), (1,)), ((), ()))
TN = (((0,), (0,)), ((), ()))
VMEM_BYTES = 58 * 1024 * 1024

BUFFERS = {
    "halo": ((2, 3, COLS, D), BF16),
    "shifted": ((2, PADDED, D), F32),
    "normed": ((FRAME, COLS, D), BF16),
    "k_win": ((FRAME, 16, 16, D), BF16),
    "v_win": ((FRAME, 16, 16, D), BF16),
    "q_tiles": ((2, 16, 64, D), BF16),
    "g_tiles": ((2, 16, 64, D), BF16),
    "attended": ((OWN, COLS, D), BF16),
    "joined": ((FRAME, COLS, 3 * D), BF16),
    "bias": ((3, 3, KEYS, LANES), F32),
    "acc": ((FRAME, PADDED, 2 * D), F32),
    "gn": ((OWN, COLS, D), F32),
    "sums": ((32, 16, 512), BF16),
    "rim_out": ((2, 3, COLS, D), BF16),
    "rim_in": ((2, 3, COLS, D), BF16),
}


def dot(a, b, dims=(((1,), (0,)), ((), ()))):
    return lax.dot_general(a, b, dims, preferred_element_type=F32)


def inverse_rms(wide):
    return lax.rsqrt(jnp.mean(wide * wide, axis=-1, keepdims=True) + 1e-6)


def windows(b, x, slot, frame_row):
    wide = x.astype(F32)
    normed = wide * inverse_rms(wide) * b.gain[...]
    b.normed[frame_row] = normed.astype(BF16)
    b.shifted[slot, 4 : 4 + COLS, :] = normed
    rows = jnp.concatenate([b.shifted[slot, 8 * j : 8 * j + 16, :] for j in range(16)], axis=0)
    kv = dot(rows.astype(BF16), b.w_in[:, D:])
    b.k_win[frame_row] = kv[:, :D].astype(BF16).reshape(16, 16, D)
    b.v_win[frame_row] = kv[:, D:].astype(BF16).reshape(16, 16, D)


def clear(b):
    b.shifted[...] = jnp.zeros_like(b.shifted)
    for r in range(3):
        b.joined[r, :, :D] = jnp.zeros((COLS, D), BF16)
        b.joined[OWN + 3 + r, :, :D] = jnp.zeros((COLS, D), BF16)

    def zero_row(r, carry):
        b.acc[r] = jnp.zeros((PADDED, 2 * D), F32)
        return carry

    lax.fori_loop(0, FRAME, zero_row, 0)


def mask(b, here, last):
    key = lax.broadcasted_iota(jnp.int32, (KEYS, LANES), 0)
    lane = lax.broadcasted_iota(jnp.int32, (KEYS, LANES), 1)
    k_row, k_col = key // 16, key % 16
    q_row, q_col = (lane % 32) // 8, lane % 8
    near = (k_row - q_row >= 0) & (k_row - q_row <= 6) & (k_col - q_col >= 1) & (k_col - q_col <= 7)
    inside = (near & ((k_row >= 3) | (here > 0)), near, near & ((k_row < 7) | (here < last)))
    for rows in range(3):
        for side, ok in enumerate((k_col >= 4, k_col >= 0, k_col < 12)):
            b.bias[rows, side] = jnp.where(inside[rows] & ok, 0.0, NEG)


def own_rows(b):
    def tile_order(pair):
        return [
            jnp.concatenate([pair[8 * j : 8 * j + 8], pair[COLS + 8 * j : COLS + 8 * j + 8]], axis=0)
            for j in range(16)
        ]

    def own_pair(i, carry):
        first = 2 * i
        half = i // 4
        place = pl.multiple_of((i % 4) * 16, 16)
        windows(b, b.tok[first], 0, first + 3)
        windows(b, b.tok[first + 1], 1, first + 4)
        both = b.normed[pl.ds(first + 3, 2)].reshape(2 * COLS, D)
        q = dot(both, b.w_in[:, :D])
        for j, tile in enumerate(tile_order(q)):
            b.q_tiles[half, j, pl.ds(place, 16), :] = (tile.astype(BF16).astype(F32) * 0.125).astype(BF16)
        g = dot(b.cot[pl.ds(first, 2)].reshape(2 * COLS, D), b.w_out[...], NT)
        for j, tile in enumerate(tile_order(g)):
            b.g_tiles[half, j, pl.ds(place, 16), :] = tile.astype(BF16)
        return carry

    lax.fori_loop(0, 8, own_pair, 0)


def halo_rows(b):
    def halo_row(r, carry):
        windows(b, b.halo[0, r], 0, r)
        windows(b, b.halo[1, r], 1, OWN + 3 + r)
        return carry

    lax.fori_loop(0, 3, halo_row, 0)


def attend(b):
    head_lane = lax.broadcasted_iota(jnp.int32, (32, D), 1) // 64

    def by_head(source, tile):
        band, j, side = tile
        rows = source[band // 2, j, 32 * (band % 2) : 32 * (band % 2) + 32]
        return jnp.concatenate(
            [jnp.where(head_lane == h, rows, jnp.zeros_like(rows)) for h in range(4)], axis=0
        )

    def of_heads(full):
        out = full[96:128]
        for h in (2, 1, 0):
            out = jnp.where(head_lane == h, full[32 * h : 32 * h + 32], out)
        return out.reshape(4, 8, D)

    def add(tile, lanes, term):
        band, j, side = tile
        b.acc[4 * band : 4 * band + 10, pl.ds(pl.multiple_of(8 * j, 8), 16), lanes] += term.reshape(10, 16, D)

    def some_tiles(tiles):
        n = range(len(tiles))
        k = [b.k_win[4 * band : 4 * band + 10, j].reshape(KEYS, D) for band, j, side in tiles]
        v = [b.v_win[4 * band : 4 * band + 10, j].reshape(KEYS, D) for band, j, side in tiles]
        q = [by_head(b.q_tiles, tile) for tile in tiles]
        g = [by_head(b.g_tiles, tile) for tile in tiles]
        s = [dot(k[i], q[i], NT) + b.bias[(0, 1, 1, 2)[u[0]], u[2]] for i, u in enumerate(tiles)]
        dp = [dot(v[i], g[i], NT) for i in n]
        e = [jnp.exp(s[i] - jnp.max(s[i], axis=0, keepdims=True)) for i in n]
        p = [e[i] * (1.0 / jnp.sum(e[i], axis=0, keepdims=True)) for i in n]
        weights = [p[i].astype(BF16) for i in n]
        for i, u in enumerate(tiles):
            add(u, slice(D, 2 * D), dot(weights[i], g[i]))
        att = [of_heads(dot(weights[i], v[i], TN)) for i in n]
        delta = [jnp.sum(p[i] * dp[i], axis=0, keepdims=True) for i in n]
        ds = [(p[i] * (dp[i] - delta[i])).astype(BF16) for i in n]
        for i, u in enumerate(tiles):
            add(u, slice(0, D), dot(ds[i], q[i]))
        dq = [of_heads(dot(ds[i], k[i], TN)) * 0.125 for i in n]
        for i in range(0, len(tiles), 2):
            band, j, side = tiles[i]
            cols = pl.ds(pl.multiple_of(8 * j, 16), 16)
            b.attended[4 * band : 4 * band + 4, cols, :] = jnp.concatenate(att[i : i + 2], axis=1).astype(BF16)
            b.joined[4 * band + 3 : 4 * band + 7, cols, :D] = jnp.concatenate(dq[i : i + 2], axis=1).astype(BF16)

    def columns(jp, carry):
        sides = jnp.where(jp == 0, 0, 1), jnp.where(jp == 7, 2, 1)
        tiles = [(band, 2 * jp + i, sides[i]) for band in range(4) for i in range(2)]
        some_tiles(tiles)
        return carry

    lax.fori_loop(0, 8, columns, 0)


def weight_sums(b):
    def key_row(r, carry):
        b.joined[r, :, D:] = b.acc[r, 4 : 4 + COLS, :].astype(BF16)
        return carry

    lax.fori_loop(0, FRAME, key_row, 0)
    g_in = dot(b.normed[...].reshape(FRAME * COLS, D), b.joined[...].reshape(FRAME * COLS, 3 * D), TN)
    g_out = dot(b.attended[...].reshape(OWN * COLS, D), b.cot[...].reshape(OWN * COLS, D), TN)
    for g in range(16):
        span = slice(16 * g, 16 * g + 16)
        b.sums[2 * g] = g_in[span, :512].astype(BF16)
        b.sums[2 * g + 1] = jnp.concatenate([g_in[span, 512:], g_out[span]], axis=1).astype(BF16)


def rim_rows(b):
    for side, first in ((0, 0), (1, OWN + 3)):
        rows = b.joined[first : first + 3].reshape(3 * COLS, 3 * D)
        b.rim_out[side] = dot(rows, b.w_in[...], NT).reshape(3, COLS, D).astype(BF16)


def own_gn(b):
    def four(i, carry):
        rows = b.joined[pl.ds(3 + 4 * i, 4)].reshape(4 * COLS, 3 * D)
        b.gn[pl.ds(4 * i, 4)] = dot(rows, b.w_in[...], NT).reshape(4, COLS, D)
        return carry

    lax.fori_loop(0, 4, four, 0)


def finish(b, row, rim=None):
    wide = b.tok[row].astype(F32)
    inv = inverse_rms(wide)
    gn = b.gn[row]
    if rim is not None:
        gn = gn + rim.astype(F32)
    gained = gn * b.gain[...]
    mean = jnp.mean(gained * wide, axis=-1, keepdims=True)
    b.gt[row] = (inv * (gained - wide * (inv * inv * mean))).astype(BF16)


def finish_rows(b, low, high):
    def body(r, carry):
        finish(b, r)
        return carry

    lax.fori_loop(low, high, body, 0)


def block_kernel(names, *refs):
    b = SimpleNamespace(**dict(zip(names, refs)))
    rows = lax.axis_index("rows")
    count = lax.axis_size("rows")
    x = lax.axis_index("dp")
    core = rows % 2
    z = (rows // 2) % 8
    y = rows // 16
    me = y * 4 + x
    before = {"rows": (rows + count - 1) % count, "dp": x}
    after = {"rows": (rows + 1) % count, "dp": x}
    partner = {"rows": rows + 1 - 2 * core, "dp": x}
    mine = 16 * core
    other = 16 - mine

    def in_plane(i):
        to_y, to_x = (y + i // 4) % 4, (x + i % 4) % 4
        return {"rows": (to_y * 8 + z) * 2 + core, "dp": to_x}, to_y * 4 + to_x

    def from_plane(i):
        return ((y + 4 - i // 4) % 4) * 4 + (x + 4 - i % 4) % 4

    def along_z(i):
        return {"rows": (y * 8 + (z + i) % 8) * 2 + core, "dp": x}

    def remote(src, dst, send, recv, where):
        return pltpu.make_async_remote_copy(
            src_ref=src, dst_ref=dst, send_sem=send, recv_sem=recv,
            device_id=where, device_id_type=pl.DeviceIdType.MESH,
        )

    barrier = pltpu.get_barrier_semaphore()

    def greet(where):
        pl.semaphore_signal(barrier, inc=1, device_id=where, device_id_type=pl.DeviceIdType.MESH)

    def greet_plane(i, carry):
        greet(in_plane(i)[0])
        return carry

    def greet_z(i, carry):
        greet(along_z(i))
        return carry

    greet(before)
    greet(after)
    greet(partner)
    lax.fori_loop(1, 16, greet_plane, 0)
    lax.fori_loop(1, 8, greet_z, 0)
    loads = [
        pltpu.make_async_copy(src, dst, b.load.at[i])
        for i, (src, dst) in enumerate(
            ((b.tok_hbm, b.tok), (b.w_in_hbm, b.w_in), (b.gain_hbm, b.gain), (b.w_out_hbm, b.w_out), (b.cot_hbm, b.cot))
        )
    ]
    for copy in loads:
        copy.start()
    clear(b)
    pl.semaphore_wait(barrier, 25)

    def halo_copies():
        return (
            remote(b.tok_hbm.at[pl.ds(OWN - 3, 3)], b.halo.at[0], b.near_send.at[0], b.near_recv.at[0], after),
            remote(b.tok_hbm.at[pl.ds(0, 3)], b.halo.at[1], b.near_send.at[1], b.near_recv.at[1], before),
        )

    def rim_copies():
        return (
            remote(b.rim_out.at[0], b.rim_in.at[1], b.near_send.at[2], b.near_recv.at[2], before),
            remote(b.rim_out.at[1], b.rim_in.at[0], b.near_send.at[3], b.near_recv.at[3], after),
        )

    def core_scatter(i):
        place = in_plane(i)[1]
        return remote(b.sums.at[other + place], b.core_got.at[i], b.core_send.at[i], b.core_recv.at[i], partner)

    def scatter(i):
        where, place = in_plane(i)
        return remote(b.paired.at[i], b.plane_got.at[i], b.plane_send.at[i], b.plane_recv.at[i], where)

    def z_share(i):
        where = along_z(i)
        return remote(b.z_all.at[z], b.z_all.at[z], b.z_send.at[i], b.z_recv.at[i], where)

    def gather(i):
        where, place = in_plane(i)
        return remote(b.full.at[mine + me], b.full.at[mine + me], b.out_send.at[i], b.out_recv.at[i], where)

    def core_gather(i):
        chunk = b.full.at[mine + from_plane(i)]
        return remote(chunk, chunk, b.last_send.at[i], b.last_recv.at[i], partner)

    def each(make, low, high, act):
        def body(i, carry):
            act(make(i))
            return carry

        lax.fori_loop(low, high, body, 0)

    def start(copy):
        copy.start()

    def wait_send(copy):
        copy.wait_send()

    def wait_recv(copy):
        copy.wait_recv()

    for copy in halo_copies():
        copy.start()
    mask(b, rows, count - 1)
    for copy in loads:
        copy.wait()
    own_rows(b)
    for copy in halo_copies():
        copy.wait_recv()
    halo_rows(b)
    attend(b)
    weight_sums(b)
    stores = [
        pltpu.make_async_copy(b.gt.at[pl.ds(low, n)], b.gt_hbm.at[pl.ds(low, n)], b.store.at[i])
        for i, (low, n) in enumerate(((3, 10), (0, 3), (OWN - 3, 3)))
    ]
    each(core_scatter, 1, 16, start)
    core_scatter(0).start()
    rim_rows(b)
    for copy in rim_copies():
        copy.start()

    def pair(i):
        core_scatter(i).wait_recv()
        return b.sums[mine + in_plane(i)[1]].astype(F32) + b.core_got[i].astype(F32)

    def pair_and_send(i, carry):
        b.paired[i] = pair(i).astype(BF16)
        scatter(i).start()
        return carry

    lax.fori_loop(1, 16, pair_and_send, 0)
    own_gn(b)

    def add_plane(i, total):
        scatter(i).wait_recv()
        return total + b.plane_got[i].astype(F32)

    total = lax.fori_loop(1, 16, add_plane, pair(0))
    b.z_all[z] = total.astype(BF16)
    each(z_share, 1, 8, start)
    finish_rows(b, 3, 13)
    stores[0].start()
    each(z_share, 1, 8, wait_recv)
    whole = b.z_all[0].astype(F32)
    for i in range(1, 8):
        whole = whole + b.z_all[i].astype(F32)
    b.full[mine + me] = whole.astype(BF16)
    each(gather, 1, 16, start)
    core_gather(0).start()
    for copy in rim_copies():
        copy.wait_recv()

    def edge(r, carry):
        finish(b, r, b.rim_in[0, r])
        finish(b, OWN - 3 + r, b.rim_in[1, r])
        return carry

    lax.fori_loop(0, 3, edge, 0)
    stores[1].start()
    stores[2].start()

    def pass_on(i, carry):
        gather(i).wait_recv()
        core_gather(i).start()
        return carry

    lax.fori_loop(1, 16, pass_on, 0)
    each(core_gather, 0, 16, wait_recv)
    for copy in halo_copies() + rim_copies():
        copy.wait_send()
    for copy in stores:
        copy.wait()
    each(core_scatter, 0, 16, wait_send)
    each(scatter, 1, 16, wait_send)
    each(z_share, 1, 8, wait_send)
    each(gather, 1, 16, wait_send)
    each(core_gather, 0, 16, wait_send)


def block(tok, cot, gain, w_in, w_out):
    vmem, hbm = pl.BlockSpec(memory_space=pltpu.VMEM), pl.BlockSpec(memory_space=pltpu.HBM)
    dma = pltpu.SemaphoreType.DMA
    outs = {"gt_hbm": ((OWN, COLS, D), BF16), "full": ((32, 16, 512), BF16)}
    slots = {
        "tok": ((OWN, COLS, D), BF16),
        "cot": ((OWN, COLS, D), BF16),
        "gain": ((1, D), F32),
        "w_in": ((D, 3 * D), BF16),
        "w_out": ((D, D), BF16),
        "gt": ((OWN, COLS, D), BF16),
        "core_got": ((16, 16, 512), BF16),
        "paired": ((16, 16, 512), BF16),
        "plane_got": ((16, 16, 512), BF16),
        "z_all": ((8, 16, 512), BF16),
    }
    sems = {
        "load": 5, "store": 3, "near_send": 4, "near_recv": 4, "core_send": 16, "core_recv": 16, "plane_send": 16, "plane_recv": 16,
        "z_send": 8, "z_recv": 8, "out_send": 16, "out_recv": 16,
        "last_send": 16, "last_recv": 16,
    }
    names = ["tok_hbm", "cot_hbm", "gain_hbm", "w_in_hbm", "w_out_hbm", *outs, *BUFFERS, *slots, *sems]

    def kernel(*refs):
        block_kernel(names, *refs)

    return pl.pallas_call(
        kernel,
        out_shape=tuple(jax.ShapeDtypeStruct(*o) for o in outs.values()),
        in_specs=[hbm] * 5,
        out_specs=(hbm, vmem),
        scratch_shapes=[
            *(pltpu.VMEM(*s) for s in BUFFERS.values()),
            *(pltpu.VMEM(*s) for s in slots.values()),
            *(dma((n,)) for n in sems.values()),
        ],
        compiler_params=pltpu.CompilerParams(
            collective_id=0, has_side_effects=True, vmem_limit_bytes=VMEM_BYTES
        ),
    )(tok, cot, gain, w_in, w_out)


def outputs(gt, full, gain, w_in, factor):
    def kernel(gt_hbm, full_hbm, gain_hbm, w_hbm, gt_out, g_in_out, g_out_out, g_gain_out,
               rows, full_ref, gain_ref, w, g_in, g_out, g_gain, sem):
        quarters = [pl.ds(4 * i, 4) for i in range(4)]
        spans = [pl.ds(64 * i, 64) for i in range(4)]

        def copies(first, pairs):
            return [pltpu.make_async_copy(src, dst, sem.at[first + i]) for i, (src, dst) in enumerate(pairs)]

        parts = copies(0, [(full_hbm.at[pl.ds(8 * i, 8)], full_ref.at[pl.ds(8 * i, 8)]) for i in range(4)])
        small = copies(4, [(w_hbm, w), (gain_hbm, gain_ref)])
        reads = copies(6, [(gt_hbm.at[r], rows.at[r]) for r in quarters])
        writes = copies(10, [(rows.at[r], gt_out.at[r]) for r in quarters])
        in_writes = copies(14, [(g_in.at[r], g_in_out.at[r]) for r in spans])
        out_writes = copies(18, [(g_out.at[r], g_out_out.at[r]) for r in spans])
        gain_write = pltpu.make_async_copy(g_gain, g_gain_out, sem.at[22])
        for copy in parts + small + reads:
            copy.start()
        for i in range(4):
            parts[i].wait()
            for g in range(4 * i, 4 * i + 4):
                span = slice(16 * g, 16 * g + 16)
                right = full_ref[2 * g + 1].astype(F32) * factor
                g_in[span, :512] = full_ref[2 * g].astype(F32) * factor
                g_in[span, 512:] = right[:, :256]
                g_out[span, :] = right[:, 256:]
            in_writes[i].start()
            out_writes[i].start()
            reads[i].wait()
            writes[i].start()
        for copy in small:
            copy.wait()
        per_row = jnp.sum(g_in[...] * w[...].astype(F32), axis=1, keepdims=True)
        g_gain[...] = jnp.transpose(jnp.broadcast_to(per_row, (D, 128)))[0:1] / gain_ref[...]
        gain_write.start()
        for copy in writes + in_writes + out_writes + [gain_write]:
            copy.wait()

    hbm = pl.BlockSpec(memory_space=pltpu.HBM)
    return pl.pallas_call(
        kernel,
        out_shape=(
            jax.ShapeDtypeStruct((OWN, COLS, D), BF16),
            jax.ShapeDtypeStruct((D, 3 * D), F32),
            jax.ShapeDtypeStruct((D, D), F32),
            jax.ShapeDtypeStruct((1, D), F32),
        ),
        in_specs=[hbm] * 4,
        out_specs=(hbm,) * 4,
        scratch_shapes=[
            pltpu.VMEM((OWN, COLS, D), BF16),
            pltpu.VMEM((32, 16, 512), BF16),
            pltpu.VMEM((1, D), F32),
            pltpu.VMEM((D, 3 * D), BF16),
            pltpu.VMEM((D, 3 * D), F32),
            pltpu.VMEM((D, D), F32),
            pltpu.VMEM((1, D), F32),
            pltpu.SemaphoreType.DMA((23,)),
        ],
        compiler_params=pltpu.CompilerParams(vmem_limit_bytes=VMEM_BYTES),
    )(gt, full, gain, w_in)


def local(tokens, norm_gain, in_weight, out_weight, cotangent):
    factor = 1.0 / math.sqrt(lax.axis_size("rows") * lax.axis_size("dp") * OWN * COLS)
    gain = norm_gain.reshape(1, D)
    gt, full = block(tokens[0], cotangent[0], gain, in_weight, out_weight)
    gt, g_in, g_out, g_gain = outputs(gt, full, gain, in_weight, factor)
    return gt[None], g_in, g_out, g_gain.reshape(D)


def solution(mesh):
    return jax.shard_map(
        local,
        mesh=mesh,
        in_specs=(P("dp", "rows", None, None), P(), P(), P(), P("dp", "rows", None, None)),
        out_specs=(P("dp", "rows", None, None), P(), P(), P()),
        check_vma=False,
    )
```

```python
import math
from types import SimpleNamespace

import jax
import jax.numpy as jnp
from jax import lax
from jax.experimental import pallas as pl
from jax.experimental.pallas import tpu as pltpu
from jax.sharding import PartitionSpec as P

F32 = jnp.float32
BF16 = jnp.bfloat16
D = 256
COLS = 128
OWN = 16
FRAME = OWN + 6
PADDED = 144
NEG = -1e30
KEYS = 160
LANES = 128
NT = (((1,), (1,)), ((), ()))
TN = (((0,), (0,)), ((), ()))
VMEM_BYTES = 58 * 1024 * 1024

BUFFERS = {
    "halo": ((2, 3, COLS, D), BF16),
    "shifted": ((2, PADDED, D), F32),
    "normed": ((FRAME, COLS, D), BF16),
    "k_win": ((FRAME, 16, 16, D), BF16),
    "v_win": ((FRAME, 16, 16, D), BF16),
    "q_tiles": ((2, 16, 64, D), BF16),
    "g_tiles": ((2, 16, 64, D), BF16),
    "attended": ((OWN, COLS, D), BF16),
    "joined": ((FRAME, COLS, 3 * D), BF16),
    "bias": ((3, 3, KEYS, LANES), F32),
    "acc": ((FRAME, PADDED, 2 * D), F32),
    "gn": ((OWN, COLS, D), F32),
    "sums": ((32, 16, 512), BF16),
    "rim_out": ((2, 3, COLS, D), BF16),
    "rim_in": ((2, 3, COLS, D), BF16),
}


def dot(a, b, dims=(((1,), (0,)), ((), ()))):
    return lax.dot_general(a, b, dims, preferred_element_type=F32)


def inverse_rms(wide):
    return lax.rsqrt(jnp.mean(wide * wide, axis=-1, keepdims=True) + 1e-6)


def windows(b, x, slot, frame_row):
    wide = x.astype(F32)
    normed = wide * inverse_rms(wide) * b.gain[...]
    b.normed[frame_row] = normed.astype(BF16)
    b.shifted[slot, 4 : 4 + COLS, :] = normed
    rows = jnp.concatenate([b.shifted[slot, 8 * j : 8 * j + 16, :] for j in range(16)], axis=0)
    kv = dot(rows.astype(BF16), b.w_in[:, D:])
    b.k_win[frame_row] = kv[:, :D].astype(BF16).reshape(16, 16, D)
    b.v_win[frame_row] = kv[:, D:].astype(BF16).reshape(16, 16, D)


def clear(b):
    b.shifted[...] = jnp.zeros_like(b.shifted)
    for r in range(3):
        b.joined[r, :, :D] = jnp.zeros((COLS, D), BF16)
        b.joined[OWN + 3 + r, :, :D] = jnp.zeros((COLS, D), BF16)

    def zero_row(r, carry):
        b.acc[r] = jnp.zeros((PADDED, 2 * D), F32)
        return carry

    lax.fori_loop(0, FRAME, zero_row, 0)


def mask(b, here, last):
    key = lax.broadcasted_iota(jnp.int32, (KEYS, LANES), 0)
    lane = lax.broadcasted_iota(jnp.int32, (KEYS, LANES), 1)
    k_row, k_col = key // 16, key % 16
    q_row, q_col = (lane % 32) // 8, lane % 8
    near = (k_row - q_row >= 0) & (k_row - q_row <= 6) & (k_col - q_col >= 1) & (k_col - q_col <= 7)
    inside = (near & ((k_row >= 3) | (here > 0)), near, near & ((k_row < 7) | (here < last)))
    for rows in range(3):
        for side, ok in enumerate((k_col >= 4, k_col >= 0, k_col < 12)):
            b.bias[rows, side] = jnp.where(inside[rows] & ok, 0.0, NEG)


def own_rows(b):
    def tile_order(pair):
        return [
            jnp.concatenate([pair[8 * j : 8 * j + 8], pair[COLS + 8 * j : COLS + 8 * j + 8]], axis=0)
            for j in range(16)
        ]

    def own_pair(i, carry):
        first = 2 * i
        half = i // 4
        place = pl.multiple_of((i % 4) * 16, 16)
        windows(b, b.tok[first], 0, first + 3)
        windows(b, b.tok[first + 1], 1, first + 4)
        both = b.normed[pl.ds(first + 3, 2)].reshape(2 * COLS, D)
        q = dot(both, b.w_in[:, :D])
        for j, tile in enumerate(tile_order(q)):
            b.q_tiles[half, j, pl.ds(place, 16), :] = (tile.astype(BF16).astype(F32) * 0.125).astype(BF16)
        g = dot(b.cot[pl.ds(first, 2)].reshape(2 * COLS, D), b.w_out[...], NT)
        for j, tile in enumerate(tile_order(g)):
            b.g_tiles[half, j, pl.ds(place, 16), :] = tile.astype(BF16)
        return carry

    lax.fori_loop(0, 8, own_pair, 0)


def halo_rows(b):
    def halo_row(r, carry):
        windows(b, b.halo[0, r], 0, r)
        windows(b, b.halo[1, r], 1, OWN + 3 + r)
        return carry

    for r in range(3):
        halo_row(r, 0)


def attend(b):
    head_lane = lax.broadcasted_iota(jnp.int32, (32, D), 1) // 64

    def by_head(source, tile):
        band, j, side = tile
        rows = source[band // 2, j, 32 * (band % 2) : 32 * (band % 2) + 32]
        return jnp.concatenate(
            [jnp.where(head_lane == h, rows, jnp.zeros_like(rows)) for h in range(4)], axis=0
        )

    def of_heads(full):
        out = full[96:128]
        for h in (2, 1, 0):
            out = jnp.where(head_lane == h, full[32 * h : 32 * h + 32], out)
        return out.reshape(4, 8, D)

    def add(tile, lanes, term):
        band, j, side = tile
        b.acc[4 * band : 4 * band + 10, pl.ds(pl.multiple_of(8 * j, 8), 16), lanes] += term.reshape(10, 16, D)

    def some_tiles(tiles):
        n = range(len(tiles))
        k = [b.k_win[4 * band : 4 * band + 10, j].reshape(KEYS, D) for band, j, side in tiles]
        v = [b.v_win[4 * band : 4 * band + 10, j].reshape(KEYS, D) for band, j, side in tiles]
        q = [by_head(b.q_tiles, tile) for tile in tiles]
        g = [by_head(b.g_tiles, tile) for tile in tiles]
        s = [dot(k[i], q[i], NT) + b.bias[(0, 1, 1, 2)[u[0]], u[2]] for i, u in enumerate(tiles)]
        dp = [dot(v[i], g[i], NT) for i in n]
        e = [jnp.exp(s[i] - jnp.max(s[i], axis=0, keepdims=True)) for i in n]
        p = [e[i] * (1.0 / jnp.sum(e[i], axis=0, keepdims=True)) for i in n]
        weights = [p[i].astype(BF16) for i in n]
        delta = [jnp.sum(p[i] * dp[i], axis=0, keepdims=True) for i in n]
        ds = [(p[i] * (dp[i] - delta[i])).astype(BF16) for i in n]
        att = [of_heads(dot(weights[i], v[i], TN)) for i in n]
        dq = [of_heads(dot(ds[i], k[i], TN)) * 0.125 for i in n]
        for i, u in enumerate(tiles):
            add(u, slice(D, 2 * D), dot(weights[i], g[i]))
        for i, u in enumerate(tiles):
            add(u, slice(0, D), dot(ds[i], q[i]))
        for i in range(0, len(tiles), 2):
            band, j, side = tiles[i]
            cols = pl.ds(pl.multiple_of(8 * j, 16), 16)
            b.attended[4 * band : 4 * band + 4, cols, :] = jnp.concatenate(att[i : i + 2], axis=1).astype(BF16)
            b.joined[4 * band + 3 : 4 * band + 7, cols, :D] = jnp.concatenate(dq[i : i + 2], axis=1).astype(BF16)

    def columns(jp, carry):
        sides = jnp.where(jp == 0, 0, 1), jnp.where(jp == 7, 2, 1)
        tiles = [(band, 2 * jp + i, sides[i]) for band in range(4) for i in range(2)]
        some_tiles(tiles)
        return carry

    lax.fori_loop(0, 8, columns, 0)


def round_keys(b):
    def key_row(r, carry):
        b.joined[r, :, D:] = b.acc[r, 4 : 4 + COLS, :].astype(BF16)
        return carry

    lax.fori_loop(0, FRAME, key_row, 0, unroll=True)


def weight_sums(b, part):
    lanes = pl.ds(pl.multiple_of(128 * part, 128), 128)
    g_in = dot(b.normed[:, :, lanes].reshape(FRAME * COLS, 128), b.joined[...].reshape(FRAME * COLS, 3 * D), TN)
    g_out = dot(b.attended[:, :, lanes].reshape(OWN * COLS, 128), b.cot[...].reshape(OWN * COLS, D), TN)
    for g in range(8):
        span = slice(16 * g, 16 * g + 16)
        b.sums[16 * part + 2 * g] = g_in[span, :512].astype(BF16)
        b.sums[16 * part + 2 * g + 1] = jnp.concatenate([g_in[span, 512:], g_out[span]], axis=1).astype(BF16)


def rim_rows(b):
    for side, first in ((0, 0), (1, OWN + 3)):
        rows = b.joined[first : first + 3].reshape(3 * COLS, 3 * D)
        b.rim_out[side] = dot(rows, b.w_in[...], NT).reshape(3, COLS, D).astype(BF16)


def own_gn(b):
    def four(i, carry):
        rows = b.joined[pl.ds(3 + 4 * i, 4)].reshape(4 * COLS, 3 * D)
        b.gn[pl.ds(4 * i, 4)] = dot(rows, b.w_in[...], NT).reshape(4, COLS, D)
        return carry

    lax.fori_loop(0, 4, four, 0)


def finish(b, row, rim=None):
    wide = b.tok[row].astype(F32)
    inv = inverse_rms(wide)
    gn = b.gn[row]
    if rim is not None:
        gn = gn + rim.astype(F32)
    gained = gn * b.gain[...]
    mean = jnp.mean(gained * wide, axis=-1, keepdims=True)
    b.gt[row] = (inv * (gained - wide * (inv * inv * mean))).astype(BF16)


def finish_rows(b, low, high):
    def body(r, carry):
        finish(b, r)
        return carry

    lax.fori_loop(low, high, body, 0)


def block_kernel(names, *refs):
    b = SimpleNamespace(**dict(zip(names, refs)))
    rows = lax.axis_index("rows")
    count = lax.axis_size("rows")
    x = lax.axis_index("dp")
    core = rows % 2
    z = (rows // 2) % 8
    y = rows // 16
    me = y * 4 + x
    before = {"rows": (rows + count - 1) % count, "dp": x}
    after = {"rows": (rows + 1) % count, "dp": x}
    partner = {"rows": rows + 1 - 2 * core, "dp": x}
    mine = 16 * core
    other = 16 - mine

    def away(i):
        return i + i // 2 - 2 * (i // 3)

    def offsets(i):
        n = (16 - i) % 16
        return away(n // 4), away(n % 4)

    def in_plane(i):
        by_y, by_x = offsets(i)
        to_y, to_x = (y + by_y) % 4, (x + by_x) % 4
        return {"rows": (to_y * 8 + z) * 2 + core, "dp": to_x}, to_y * 4 + to_x

    def from_plane(i):
        by_y, by_x = offsets(i)
        return ((y + 4 - by_y) % 4) * 4 + (x + 4 - by_x) % 4

    def along_z(i):
        by_z = 4 + (i // 2) * (2 * (i % 2) - 1)
        return {"rows": (y * 8 + (z + by_z) % 8) * 2 + core, "dp": x}

    def remote(src, dst, send, recv, where):
        return pltpu.make_async_remote_copy(
            src_ref=src, dst_ref=dst, send_sem=send, recv_sem=recv,
            device_id=where, device_id_type=pl.DeviceIdType.MESH,
        )

    barrier = pltpu.get_barrier_semaphore()

    def greet(where):
        pl.semaphore_signal(barrier, inc=1, device_id=where, device_id_type=pl.DeviceIdType.MESH)

    def greet_plane(i, carry):
        greet(in_plane(i)[0])
        return carry

    def greet_z(i, carry):
        greet(along_z(i))
        return carry

    greet(before)
    greet(after)
    greet(partner)
    lax.fori_loop(1, 16, greet_plane, 0)
    lax.fori_loop(1, 8, greet_z, 0)
    loads = [
        pltpu.make_async_copy(src, dst, b.load.at[i])
        for i, (src, dst) in enumerate(
            ((b.tok_hbm, b.tok), (b.w_in_hbm, b.w_in), (b.gain_hbm, b.gain), (b.w_out_hbm, b.w_out), (b.cot_hbm, b.cot))
        )
    ]
    for copy in loads:
        copy.start()
    clear(b)
    pl.semaphore_wait(barrier, 25)

    def halo_copies():
        return (
            remote(b.tok_hbm.at[pl.ds(OWN - 3, 3)], b.halo.at[0], b.near_send.at[0], b.near_recv.at[0], after),
            remote(b.tok_hbm.at[pl.ds(0, 3)], b.halo.at[1], b.near_send.at[1], b.near_recv.at[1], before),
        )

    def rim_copies():
        return (
            remote(b.rim_out.at[0], b.rim_in.at[1], b.near_send.at[2], b.near_recv.at[2], before),
            remote(b.rim_out.at[1], b.rim_in.at[0], b.near_send.at[3], b.near_recv.at[3], after),
        )

    def core_scatter(i):
        place = in_plane(i)[1]
        return remote(b.sums.at[other + place], b.core_got.at[i], b.core_send.at[i], b.core_recv.at[i], partner)

    def scatter(i):
        where, place = in_plane(i)
        return remote(b.paired.at[i], b.plane_got.at[i], b.plane_send.at[i], b.plane_recv.at[i], where)

    def z_share(i):
        where = along_z(i)
        return remote(b.z_all.at[z], b.z_all.at[z], b.z_send.at[i], b.z_recv.at[i], where)

    def gather(i):
        where, place = in_plane(i)
        return remote(b.full.at[mine + me], b.full.at[mine + me], b.out_send.at[i], b.out_recv.at[i], where)

    def core_gather(i):
        chunk = b.full.at[mine + from_plane(i)]
        return remote(chunk, chunk, b.last_send.at[i], b.last_recv.at[i], partner)

    def each(make, low, high, act):
        def body(i, carry):
            act(make(i))
            return carry

        lax.fori_loop(low, high, body, 0)

    def start(copy):
        copy.start()

    def wait_send(copy):
        copy.wait_send()

    def wait_recv(copy):
        copy.wait_recv()

    for copy in halo_copies():
        copy.start()
    mask(b, rows, count - 1)
    for copy in loads:
        copy.wait()
    own_rows(b)
    for copy in halo_copies():
        copy.wait_recv()
    halo_rows(b)
    attend(b)
    round_keys(b)
    weight_sums(b, 1 - core)
    stores = [
        pltpu.make_async_copy(b.gt.at[pl.ds(low, n)], b.gt_hbm.at[pl.ds(low, n)], b.store.at[i])
        for i, (low, n) in enumerate(((3, 10), (0, 3), (OWN - 3, 3)))
    ]
    each(core_scatter, 1, 16, start)
    core_scatter(0).start()
    weight_sums(b, core)
    rim_rows(b)
    for copy in rim_copies():
        copy.start()

    def pair(i):
        core_scatter(i).wait_recv()
        return b.sums[mine + in_plane(i)[1]].astype(F32) + b.core_got[i].astype(F32)

    def pair_and_send(i, carry):
        b.paired[i] = pair(i).astype(BF16)
        scatter(i).start()
        return carry

    lax.fori_loop(1, 16, pair_and_send, 0)
    own_gn(b)

    def add_plane(i, total):
        scatter(i).wait_recv()
        return total + b.plane_got[i].astype(F32)

    total = lax.fori_loop(1, 16, add_plane, pair(0))
    b.z_all[z] = total.astype(BF16)
    each(z_share, 1, 8, start)
    finish_rows(b, 3, 13)
    stores[0].start()
    each(z_share, 1, 8, wait_recv)
    whole = b.z_all[0].astype(F32)
    for i in range(1, 8):
        whole = whole + b.z_all[i].astype(F32)
    b.full[mine + me] = whole.astype(BF16)
    each(gather, 1, 16, start)
    core_gather(0).start()
    for copy in rim_copies():
        copy.wait_recv()

    def edge(r, carry):
        finish(b, r, b.rim_in[0, r])
        finish(b, OWN - 3 + r, b.rim_in[1, r])
        return carry

    lax.fori_loop(0, 3, edge, 0)
    stores[1].start()
    stores[2].start()

    def pass_on(i, carry):
        gather(16 - i).wait_recv()
        core_gather(16 - i).start()
        return carry

    lax.fori_loop(1, 16, pass_on, 0)
    each(core_gather, 0, 16, wait_recv)
    for copy in halo_copies() + rim_copies():
        copy.wait_send()
    for copy in stores:
        copy.wait()
    each(core_scatter, 0, 16, wait_send)
    each(scatter, 1, 16, wait_send)
    each(z_share, 1, 8, wait_send)
    each(gather, 1, 16, wait_send)
    each(core_gather, 0, 16, wait_send)


def block(tok, cot, gain, w_in, w_out):
    vmem, hbm = pl.BlockSpec(memory_space=pltpu.VMEM), pl.BlockSpec(memory_space=pltpu.HBM)
    dma = pltpu.SemaphoreType.DMA
    outs = {"gt_hbm": ((OWN, COLS, D), BF16), "full": ((32, 16, 512), BF16)}
    slots = {
        "tok": ((OWN, COLS, D), BF16),
        "cot": ((OWN, COLS, D), BF16),
        "gain": ((1, D), F32),
        "w_in": ((D, 3 * D), BF16),
        "w_out": ((D, D), BF16),
        "gt": ((OWN, COLS, D), BF16),
        "core_got": ((16, 16, 512), BF16),
        "paired": ((16, 16, 512), BF16),
        "plane_got": ((16, 16, 512), BF16),
        "z_all": ((8, 16, 512), BF16),
    }
    sems = {
        "load": 5, "store": 3, "near_send": 4, "near_recv": 4, "core_send": 16, "core_recv": 16, "plane_send": 16, "plane_recv": 16,
        "z_send": 8, "z_recv": 8, "out_send": 16, "out_recv": 16,
        "last_send": 16, "last_recv": 16,
    }
    names = ["tok_hbm", "cot_hbm", "gain_hbm", "w_in_hbm", "w_out_hbm", *outs, *BUFFERS, *slots, *sems]

    def kernel(*refs):
        block_kernel(names, *refs)

    return pl.pallas_call(
        kernel,
        out_shape=tuple(jax.ShapeDtypeStruct(*o) for o in outs.values()),
        in_specs=[hbm] * 5,
        out_specs=(hbm, vmem),
        scratch_shapes=[
            *(pltpu.VMEM(*s) for s in BUFFERS.values()),
            *(pltpu.VMEM(*s) for s in slots.values()),
            *(dma((n,)) for n in sems.values()),
        ],
        compiler_params=pltpu.CompilerParams(
            collective_id=0, has_side_effects=True, vmem_limit_bytes=VMEM_BYTES
        ),
    )(tok, cot, gain, w_in, w_out)


def outputs(gt, full, gain, w_in, factor):
    def kernel(gt_hbm, full_hbm, gain_hbm, w_hbm, gt_out, g_in_out, g_out_out, g_gain_out,
               rows, full_ref, gain_ref, w, g_in, g_out, g_gain, sem):
        quarters = [pl.ds(4 * i, 4) for i in range(4)]
        spans = [pl.ds(64 * i, 64) for i in range(4)]

        def copies(first, pairs):
            return [pltpu.make_async_copy(src, dst, sem.at[first + i]) for i, (src, dst) in enumerate(pairs)]

        parts = copies(0, [(full_hbm.at[pl.ds(8 * i, 8)], full_ref.at[pl.ds(8 * i, 8)]) for i in range(4)])
        small = copies(4, [(w_hbm, w), (gain_hbm, gain_ref)])
        reads = copies(6, [(gt_hbm.at[r], rows.at[r]) for r in quarters])
        writes = copies(10, [(rows.at[r], gt_out.at[r]) for r in quarters])
        in_writes = copies(14, [(g_in.at[r], g_in_out.at[r]) for r in spans])
        out_writes = copies(18, [(g_out.at[r], g_out_out.at[r]) for r in spans])
        gain_write = pltpu.make_async_copy(g_gain, g_gain_out, sem.at[22])
        for copy in parts + small + reads:
            copy.start()
        for i in range(4):
            parts[i].wait()
            for g in range(4 * i, 4 * i + 4):
                span = slice(16 * g, 16 * g + 16)
                right = full_ref[2 * g + 1].astype(F32) * factor
                g_in[span, :512] = full_ref[2 * g].astype(F32) * factor
                g_in[span, 512:] = right[:, :256]
                g_out[span, :] = right[:, 256:]
            in_writes[i].start()
            out_writes[i].start()
            reads[i].wait()
            writes[i].start()
        for copy in small:
            copy.wait()
        per_row = jnp.sum(g_in[...] * w[...].astype(F32), axis=1, keepdims=True)
        g_gain[...] = jnp.transpose(jnp.broadcast_to(per_row, (D, 128)))[0:1] / gain_ref[...]
        gain_write.start()
        for copy in writes + in_writes + out_writes + [gain_write]:
            copy.wait()

    hbm = pl.BlockSpec(memory_space=pltpu.HBM)
    return pl.pallas_call(
        kernel,
        out_shape=(
            jax.ShapeDtypeStruct((OWN, COLS, D), BF16),
            jax.ShapeDtypeStruct((D, 3 * D), F32),
            jax.ShapeDtypeStruct((D, D), F32),
            jax.ShapeDtypeStruct((1, D), F32),
        ),
        in_specs=[hbm] * 4,
        out_specs=(hbm,) * 4,
        scratch_shapes=[
            pltpu.VMEM((OWN, COLS, D), BF16),
            pltpu.VMEM((32, 16, 512), BF16),
            pltpu.VMEM((1, D), F32),
            pltpu.VMEM((D, 3 * D), BF16),
            pltpu.VMEM((D, 3 * D), F32),
            pltpu.VMEM((D, D), F32),
            pltpu.VMEM((1, D), F32),
            pltpu.SemaphoreType.DMA((23,)),
        ],
        compiler_params=pltpu.CompilerParams(vmem_limit_bytes=VMEM_BYTES),
    )(gt, full, gain, w_in)


def local(tokens, norm_gain, in_weight, out_weight, cotangent):
    factor = 1.0 / math.sqrt(lax.axis_size("rows") * lax.axis_size("dp") * OWN * COLS)
    gain = norm_gain.reshape(1, D)
    gt, full = block(tokens[0], cotangent[0], gain, in_weight, out_weight)
    gt, g_in, g_out, g_gain = outputs(gt, full, gain, in_weight, factor)
    return gt[None], g_in, g_out, g_gain.reshape(D)


def solution(mesh):
    return jax.shard_map(
        local,
        mesh=mesh,
        in_specs=(P("dp", "rows", None, None), P(), P(), P(), P("dp", "rows", None, None)),
        out_specs=(P("dp", "rows", None, None), P(), P(), P()),
        check_vma=False,
    )
```

```python
import math
from types import SimpleNamespace

import jax
import jax.numpy as jnp
from jax import lax
from jax.experimental import pallas as pl
from jax.experimental.pallas import tpu as pltpu
from jax.sharding import PartitionSpec as P

F32 = jnp.float32
BF16 = jnp.bfloat16
D = 256
COLS = 128
OWN = 16
FRAME = OWN + 6
PADDED = 144
NEG = -1e30
KEYS = 160
LANES = 128
NT = (((1,), (1,)), ((), ()))
TN = (((0,), (0,)), ((), ()))
VMEM_BYTES = 58 * 1024 * 1024

BUFFERS = {
    "halo": ((2, 3, COLS, D), BF16),
    "shifted": ((2, PADDED, D), F32),
    "normed": ((FRAME, COLS, D), BF16),
    "k_win": ((FRAME, 16, 16, D), BF16),
    "v_win": ((FRAME, 16, 16, D), BF16),
    "q_tiles": ((2, 16, 64, D), BF16),
    "g_tiles": ((2, 16, 64, D), BF16),
    "attended": ((OWN, COLS, D), BF16),
    "joined": ((FRAME, COLS, 3 * D), BF16),
    "bias": ((3, 3, KEYS, LANES), F32),
    "acc": ((FRAME, PADDED, 2 * D), F32),
    "gn": ((OWN, COLS, D), F32),
    "sums": ((32, 16, 512), BF16),
    "rim_out": ((2, 3, COLS, D), BF16),
    "rim_in": ((2, 3, COLS, D), BF16),
}


def dot(a, b, dims=(((1,), (0,)), ((), ()))):
    return lax.dot_general(a, b, dims, preferred_element_type=F32)


def inverse_rms(wide):
    return lax.rsqrt(jnp.mean(wide * wide, axis=-1, keepdims=True) + 1e-6)


def windows(b, x, slot, frame_row):
    wide = x.astype(F32)
    normed = wide * inverse_rms(wide) * b.gain[...]
    b.normed[frame_row] = normed.astype(BF16)
    b.shifted[slot, 4 : 4 + COLS, :] = normed
    rows = jnp.concatenate([b.shifted[slot, 8 * j : 8 * j + 16, :] for j in range(16)], axis=0)
    kv = dot(rows.astype(BF16), b.w_in[:, D:])
    b.k_win[frame_row] = kv[:, :D].astype(BF16).reshape(16, 16, D)
    b.v_win[frame_row] = kv[:, D:].astype(BF16).reshape(16, 16, D)


def clear(b):
    b.shifted[...] = jnp.zeros_like(b.shifted)
    for r in range(3):
        b.joined[r, :, :D] = jnp.zeros((COLS, D), BF16)
        b.joined[OWN + 3 + r, :, :D] = jnp.zeros((COLS, D), BF16)

    def zero_row(r, carry):
        b.acc[r] = jnp.zeros((PADDED, 2 * D), F32)
        return carry

    lax.fori_loop(0, FRAME, zero_row, 0)


def mask(b, here, last):
    key = lax.broadcasted_iota(jnp.int32, (KEYS, LANES), 0)
    lane = lax.broadcasted_iota(jnp.int32, (KEYS, LANES), 1)
    k_row, k_col = key // 16, key % 16
    q_row, q_col = (lane % 32) // 8, lane % 8
    near = (k_row - q_row >= 0) & (k_row - q_row <= 6) & (k_col - q_col >= 1) & (k_col - q_col <= 7)
    inside = (near & ((k_row >= 3) | (here > 0)), near, near & ((k_row < 7) | (here < last)))
    for rows in range(3):
        for side, ok in enumerate((k_col >= 4, k_col >= 0, k_col < 12)):
            b.bias[rows, side] = jnp.where(inside[rows] & ok, 0.0, NEG)


def own_rows(b):
    def tile_order(pair):
        return [
            jnp.concatenate([pair[8 * j : 8 * j + 8], pair[COLS + 8 * j : COLS + 8 * j + 8]], axis=0)
            for j in range(16)
        ]

    def own_pair(i, carry):
        first = 2 * i
        half = i // 4
        place = pl.multiple_of((i % 4) * 16, 16)
        windows(b, b.tok[first], 0, first + 3)
        windows(b, b.tok[first + 1], 1, first + 4)
        both = b.normed[pl.ds(first + 3, 2)].reshape(2 * COLS, D)
        q = dot(both, b.w_in[:, :D])
        for j, tile in enumerate(tile_order(q)):
            b.q_tiles[half, j, pl.ds(place, 16), :] = (tile.astype(BF16).astype(F32) * 0.125).astype(BF16)
        g = dot(b.cot[pl.ds(first, 2)].reshape(2 * COLS, D), b.w_out[...], NT)
        for j, tile in enumerate(tile_order(g)):
            b.g_tiles[half, j, pl.ds(place, 16), :] = tile.astype(BF16)
        return carry

    lax.fori_loop(0, 8, own_pair, 0)


def halo_rows(b):
    def halo_row(r, carry):
        windows(b, b.halo[0, r], 0, r)
        windows(b, b.halo[1, r], 1, OWN + 3 + r)
        return carry

    for r in range(3):
        halo_row(r, 0)


def attend(b):
    head_lane = lax.broadcasted_iota(jnp.int32, (32, D), 1) // 64

    def by_head(source, tile):
        band, j, side = tile
        rows = source[band // 2, j, 32 * (band % 2) : 32 * (band % 2) + 32]
        return jnp.concatenate(
            [jnp.where(head_lane == h, rows, jnp.zeros_like(rows)) for h in range(4)], axis=0
        )

    def of_heads(full):
        out = full[96:128]
        for h in (2, 1, 0):
            out = jnp.where(head_lane == h, full[32 * h : 32 * h + 32], out)
        return out.reshape(4, 8, D)

    def add(tile, lanes, term):
        band, j, side = tile
        b.acc[4 * band : 4 * band + 10, pl.ds(pl.multiple_of(8 * j, 8), 16), lanes] += term.reshape(10, 16, D)

    def some_tiles(tiles):
        n = range(len(tiles))
        k = [b.k_win[4 * band : 4 * band + 10, j].reshape(KEYS, D) for band, j, side in tiles]
        v = [b.v_win[4 * band : 4 * band + 10, j].reshape(KEYS, D) for band, j, side in tiles]
        q = [by_head(b.q_tiles, tile) for tile in tiles]
        g = [by_head(b.g_tiles, tile) for tile in tiles]
        s = [dot(k[i], q[i], NT) + b.bias[(0, 1, 1, 2)[u[0]], u[2]] for i, u in enumerate(tiles)]
        dp = [dot(v[i], g[i], NT) for i in n]
        e = [jnp.exp(s[i] - jnp.max(s[i], axis=0, keepdims=True)) for i in n]
        p = [e[i] * (1.0 / jnp.sum(e[i], axis=0, keepdims=True)) for i in n]
        weights = [p[i].astype(BF16) for i in n]
        delta = [jnp.sum(p[i] * dp[i], axis=0, keepdims=True) for i in n]
        ds = [(p[i] * (dp[i] - delta[i])).astype(BF16) for i in n]
        att = [of_heads(dot(weights[i], v[i], TN)) for i in n]
        dq = [of_heads(dot(ds[i], k[i], TN)) * 0.125 for i in n]
        for i, u in enumerate(tiles):
            add(u, slice(D, 2 * D), dot(weights[i], g[i]))
        for i, u in enumerate(tiles):
            add(u, slice(0, D), dot(ds[i], q[i]))
        for i in range(0, len(tiles), 2):
            band, j, side = tiles[i]
            cols = pl.ds(pl.multiple_of(8 * j, 16), 16)
            b.attended[4 * band : 4 * band + 4, cols, :] = jnp.concatenate(att[i : i + 2], axis=1).astype(BF16)
            b.joined[4 * band + 3 : 4 * band + 7, cols, :D] = jnp.concatenate(dq[i : i + 2], axis=1).astype(BF16)

    def columns(jp, carry):
        sides = jnp.where(jp == 0, 0, 1), jnp.where(jp == 7, 2, 1)
        tiles = [(band, 2 * jp + i, sides[i]) for band in range(4) for i in range(2)]
        some_tiles(tiles)
        return carry

    lax.fori_loop(0, 8, columns, 0, unroll=2)


def round_keys(b):
    def key_row(r, carry):
        b.joined[r, :, D:] = b.acc[r, 4 : 4 + COLS, :].astype(BF16)
        return carry

    lax.fori_loop(0, FRAME, key_row, 0, unroll=True)


def weight_sums(b, part):
    lanes = pl.ds(pl.multiple_of(128 * part, 128), 128)
    g_in = dot(b.normed[:, :, lanes].reshape(FRAME * COLS, 128), b.joined[...].reshape(FRAME * COLS, 3 * D), TN)
    g_out = dot(b.attended[:, :, lanes].reshape(OWN * COLS, 128), b.cot[...].reshape(OWN * COLS, D), TN)
    for g in range(8):
        span = slice(16 * g, 16 * g + 16)
        b.sums[16 * part + 2 * g] = g_in[span, :512].astype(BF16)
        b.sums[16 * part + 2 * g + 1] = jnp.concatenate([g_in[span, 512:], g_out[span]], axis=1).astype(BF16)


def rim_rows(b):
    for side, first in ((0, 0), (1, OWN + 3)):
        rows = b.joined[first : first + 3].reshape(3 * COLS, 3 * D)
        b.rim_out[side] = dot(rows, b.w_in[...], NT).reshape(3, COLS, D).astype(BF16)


def own_gn(b):
    def four(i, carry):
        rows = b.joined[pl.ds(3 + 4 * i, 4)].reshape(4 * COLS, 3 * D)
        b.gn[pl.ds(4 * i, 4)] = dot(rows, b.w_in[...], NT).reshape(4, COLS, D)
        return carry

    lax.fori_loop(0, 4, four, 0)


def finish(b, row, rim=None):
    wide = b.tok[row].astype(F32)
    inv = inverse_rms(wide)
    gn = b.gn[row]
    if rim is not None:
        gn = gn + rim.astype(F32)
    gained = gn * b.gain[...]
    mean = jnp.mean(gained * wide, axis=-1, keepdims=True)
    b.gt[row] = (inv * (gained - wide * (inv * inv * mean))).astype(BF16)


def finish_rows(b, low, high):
    def body(r, carry):
        finish(b, r)
        return carry

    lax.fori_loop(low, high, body, 0)


def block_kernel(names, *refs):
    b = SimpleNamespace(**dict(zip(names, refs)))
    rows = lax.axis_index("rows")
    count = lax.axis_size("rows")
    x = lax.axis_index("dp")
    core = rows % 2
    z = (rows // 2) % 8
    y = rows // 16
    me = y * 4 + x
    before = {"rows": (rows + count - 1) % count, "dp": x}
    after = {"rows": (rows + 1) % count, "dp": x}
    partner = {"rows": rows + 1 - 2 * core, "dp": x}
    mine = 16 * core
    other = 16 - mine

    def away(i):
        return i + i // 2 - 2 * (i // 3)

    def offsets(i):
        n = (16 - i) % 16
        return away(n // 4), away(n % 4)

    def in_plane(i):
        by_y, by_x = offsets(i)
        to_y, to_x = (y + by_y) % 4, (x + by_x) % 4
        return {"rows": (to_y * 8 + z) * 2 + core, "dp": to_x}, to_y * 4 + to_x

    def from_plane(i):
        by_y, by_x = offsets(i)
        return ((y + 4 - by_y) % 4) * 4 + (x + 4 - by_x) % 4

    def along_z(i):
        by_z = 4 + (i // 2) * (2 * (i % 2) - 1)
        return {"rows": (y * 8 + (z + by_z) % 8) * 2 + core, "dp": x}

    def remote(src, dst, send, recv, where):
        return pltpu.make_async_remote_copy(
            src_ref=src, dst_ref=dst, send_sem=send, recv_sem=recv,
            device_id=where, device_id_type=pl.DeviceIdType.MESH,
        )

    loads = [
        pltpu.make_async_copy(src, dst, b.load.at[i])
        for i, (src, dst) in enumerate(
            ((b.tok_hbm, b.tok), (b.w_in_hbm, b.w_in), (b.gain_hbm, b.gain), (b.w_out_hbm, b.w_out), (b.cot_hbm, b.cot))
        )
    ]
    for copy in loads:
        copy.start()
    barrier = pltpu.get_barrier_semaphore()

    def greet(where):
        pl.semaphore_signal(barrier, inc=1, device_id=where, device_id_type=pl.DeviceIdType.MESH)

    def greet_plane(i, carry):
        greet(in_plane(i)[0])
        return carry

    def greet_z(i, carry):
        greet(along_z(i))
        return carry

    greet(before)
    greet(after)
    greet(partner)
    lax.fori_loop(1, 16, greet_plane, 0)
    lax.fori_loop(1, 8, greet_z, 0)
    pl.semaphore_wait(barrier, 25)

    def halo_copies():
        return (
            remote(b.tok_hbm.at[pl.ds(OWN - 3, 3)], b.halo.at[0], b.near_send.at[0], b.near_recv.at[0], after),
            remote(b.tok_hbm.at[pl.ds(0, 3)], b.halo.at[1], b.near_send.at[1], b.near_recv.at[1], before),
        )

    def rim_copies():
        return (
            remote(b.rim_out.at[0], b.rim_in.at[1], b.near_send.at[2], b.near_recv.at[2], before),
            remote(b.rim_out.at[1], b.rim_in.at[0], b.near_send.at[3], b.near_recv.at[3], after),
        )

    def core_scatter(i):
        place = in_plane(i)[1]
        return remote(b.sums.at[other + place], b.core_got.at[i], b.core_send.at[i], b.core_recv.at[i], partner)

    def scatter(i):
        where, place = in_plane(i)
        return remote(b.paired.at[i], b.plane_got.at[i], b.plane_send.at[i], b.plane_recv.at[i], where)

    def z_share(i):
        where = along_z(i)
        return remote(b.z_all.at[z], b.z_all.at[z], b.z_send.at[i], b.z_recv.at[i], where)

    def gather(i):
        where, place = in_plane(i)
        return remote(b.full.at[mine + me], b.full.at[mine + me], b.out_send.at[i], b.out_recv.at[i], where)

    def core_gather(i):
        chunk = b.full.at[mine + from_plane(i)]
        return remote(chunk, chunk, b.last_send.at[i], b.last_recv.at[i], partner)

    def each(make, low, high, act):
        def body(i, carry):
            act(make(i))
            return carry

        lax.fori_loop(low, high, body, 0)

    def start(copy):
        copy.start()

    def wait_send(copy):
        copy.wait_send()

    def wait_recv(copy):
        copy.wait_recv()

    for copy in halo_copies():
        copy.start()
    clear(b)
    mask(b, rows, count - 1)
    for copy in loads:
        copy.wait()
    own_rows(b)
    for copy in halo_copies():
        copy.wait_recv()
    halo_rows(b)
    attend(b)
    round_keys(b)
    weight_sums(b, 1 - core)
    stores = [
        pltpu.make_async_copy(b.gt.at[pl.ds(low, n)], b.gt_hbm.at[pl.ds(low, n)], b.store.at[i])
        for i, (low, n) in enumerate(((3, 10), (0, 3), (OWN - 3, 3)))
    ]
    each(core_scatter, 1, 16, start)
    core_scatter(0).start()
    weight_sums(b, core)
    rim_rows(b)
    for copy in rim_copies():
        copy.start()

    def pair(i):
        core_scatter(i).wait_recv()
        return b.sums[mine + in_plane(i)[1]].astype(F32) + b.core_got[i].astype(F32)

    def pair_and_send(i, carry):
        b.paired[i] = pair(i).astype(BF16)
        scatter(i).start()
        return carry

    lax.fori_loop(1, 16, pair_and_send, 0)
    own_gn(b)

    def add_plane(i, total):
        scatter(i).wait_recv()
        return total + b.plane_got[i].astype(F32)

    total = lax.fori_loop(1, 16, add_plane, pair(0))
    b.z_all[z] = total.astype(BF16)
    each(z_share, 1, 8, start)
    finish_rows(b, 3, 13)
    stores[0].start()
    each(z_share, 1, 8, wait_recv)
    whole = b.z_all[0].astype(F32)
    for i in range(1, 8):
        whole = whole + b.z_all[i].astype(F32)
    b.full[mine + me] = whole.astype(BF16)
    each(gather, 1, 16, start)
    core_gather(0).start()
    for copy in rim_copies():
        copy.wait_recv()

    def edge(r, carry):
        finish(b, r, b.rim_in[0, r])
        finish(b, OWN - 3 + r, b.rim_in[1, r])
        return carry

    lax.fori_loop(0, 3, edge, 0)
    stores[1].start()
    stores[2].start()
    for copy in halo_copies() + rim_copies():
        copy.wait_send()
    each(core_scatter, 0, 16, wait_send)
    each(scatter, 1, 16, wait_send)
    each(z_share, 1, 8, wait_send)

    def pass_on(i, carry):
        gather(16 - i).wait_recv()
        core_gather(16 - i).start()
        return carry

    lax.fori_loop(1, 16, pass_on, 0)
    each(core_gather, 0, 16, wait_recv)
    for copy in stores:
        copy.wait()
    each(gather, 1, 16, wait_send)
    each(core_gather, 0, 16, wait_send)


def block(tok, cot, gain, w_in, w_out):
    vmem, hbm = pl.BlockSpec(memory_space=pltpu.VMEM), pl.BlockSpec(memory_space=pltpu.HBM)
    dma = pltpu.SemaphoreType.DMA
    outs = {"gt_hbm": ((OWN, COLS, D), BF16), "full": ((32, 16, 512), BF16)}
    slots = {
        "tok": ((OWN, COLS, D), BF16),
        "cot": ((OWN, COLS, D), BF16),
        "gain": ((1, D), F32),
        "w_in": ((D, 3 * D), BF16),
        "w_out": ((D, D), BF16),
        "gt": ((OWN, COLS, D), BF16),
        "core_got": ((16, 16, 512), BF16),
        "paired": ((16, 16, 512), BF16),
        "plane_got": ((16, 16, 512), BF16),
        "z_all": ((8, 16, 512), BF16),
    }
    sems = {
        "load": 5, "store": 3, "near_send": 4, "near_recv": 4, "core_send": 16, "core_recv": 16, "plane_send": 16, "plane_recv": 16,
        "z_send": 8, "z_recv": 8, "out_send": 16, "out_recv": 16,
        "last_send": 16, "last_recv": 16,
    }
    names = ["tok_hbm", "cot_hbm", "gain_hbm", "w_in_hbm", "w_out_hbm", *outs, *BUFFERS, *slots, *sems]

    def kernel(*refs):
        block_kernel(names, *refs)

    return pl.pallas_call(
        kernel,
        out_shape=tuple(jax.ShapeDtypeStruct(*o) for o in outs.values()),
        in_specs=[hbm] * 5,
        out_specs=(hbm, vmem),
        scratch_shapes=[
            *(pltpu.VMEM(*s) for s in BUFFERS.values()),
            *(pltpu.VMEM(*s) for s in slots.values()),
            *(dma((n,)) for n in sems.values()),
        ],
        compiler_params=pltpu.CompilerParams(
            collective_id=0, has_side_effects=True, vmem_limit_bytes=VMEM_BYTES
        ),
    )(tok, cot, gain, w_in, w_out)


def outputs(gt, full, gain, w_in, factor):
    def kernel(gt_hbm, full_hbm, gain_hbm, w_hbm, gt_out, g_in_out, g_out_out, g_gain_out,
               rows, full_ref, gain_ref, w, g_in, g_out, g_gain, sem):
        quarters = [pl.ds(4 * i, 4) for i in range(4)]
        spans = [pl.ds(64 * i, 64) for i in range(4)]

        def copies(first, pairs):
            return [pltpu.make_async_copy(src, dst, sem.at[first + i]) for i, (src, dst) in enumerate(pairs)]

        parts = copies(0, [(full_hbm.at[pl.ds(8 * i, 8)], full_ref.at[pl.ds(8 * i, 8)]) for i in range(4)])
        small = copies(4, [(w_hbm, w), (gain_hbm, gain_ref)])
        reads = copies(6, [(gt_hbm.at[r], rows.at[r]) for r in quarters])
        writes = copies(10, [(rows.at[r], gt_out.at[r]) for r in quarters])
        in_writes = copies(14, [(g_in.at[r], g_in_out.at[r]) for r in spans])
        out_writes = copies(18, [(g_out.at[r], g_out_out.at[r]) for r in spans])
        gain_write = pltpu.make_async_copy(g_gain, g_gain_out, sem.at[22])
        for copy in parts + small + reads:
            copy.start()
        for i in range(4):
            parts[i].wait()
            for g in range(4 * i, 4 * i + 4):
                span = slice(16 * g, 16 * g + 16)
                right = full_ref[2 * g + 1].astype(F32) * factor
                g_in[span, :512] = full_ref[2 * g].astype(F32) * factor
                g_in[span, 512:] = right[:, :256]
                g_out[span, :] = right[:, 256:]
            in_writes[i].start()
            out_writes[i].start()
            reads[i].wait()
            writes[i].start()
        for copy in small:
            copy.wait()
        per_row = jnp.sum(g_in[...] * w[...].astype(F32), axis=1, keepdims=True)
        g_gain[...] = jnp.transpose(jnp.broadcast_to(per_row, (D, 128)))[0:1] / gain_ref[...]
        gain_write.start()
        for copy in writes + in_writes + out_writes + [gain_write]:
            copy.wait()

    hbm = pl.BlockSpec(memory_space=pltpu.HBM)
    return pl.pallas_call(
        kernel,
        out_shape=(
            jax.ShapeDtypeStruct((OWN, COLS, D), BF16),
            jax.ShapeDtypeStruct((D, 3 * D), F32),
            jax.ShapeDtypeStruct((D, D), F32),
            jax.ShapeDtypeStruct((1, D), F32),
        ),
        in_specs=[hbm] * 4,
        out_specs=(hbm,) * 4,
        scratch_shapes=[
            pltpu.VMEM((OWN, COLS, D), BF16),
            pltpu.VMEM((32, 16, 512), BF16),
            pltpu.VMEM((1, D), F32),
            pltpu.VMEM((D, 3 * D), BF16),
            pltpu.VMEM((D, 3 * D), F32),
            pltpu.VMEM((D, D), F32),
            pltpu.VMEM((1, D), F32),
            pltpu.SemaphoreType.DMA((23,)),
        ],
        compiler_params=pltpu.CompilerParams(vmem_limit_bytes=VMEM_BYTES),
    )(gt, full, gain, w_in)


def local(tokens, norm_gain, in_weight, out_weight, cotangent):
    factor = 1.0 / math.sqrt(lax.axis_size("rows") * lax.axis_size("dp") * OWN * COLS)
    gain = norm_gain.reshape(1, D)
    gt, full = block(tokens[0], cotangent[0], gain, in_weight, out_weight)
    gt, g_in, g_out, g_gain = outputs(gt, full, gain, in_weight, factor)
    return gt[None], g_in, g_out, g_gain.reshape(D)


def solution(mesh):
    return jax.shard_map(
        local,
        mesh=mesh,
        in_specs=(P("dp", "rows", None, None), P(), P(), P(), P("dp", "rows", None, None)),
        out_specs=(P("dp", "rows", None, None), P(), P(), P()),
        check_vma=False,
    )
```

```python
import math
from types import SimpleNamespace

import jax
import jax.numpy as jnp
from jax import lax
from jax.experimental import pallas as pl
from jax.experimental.pallas import tpu as pltpu
from jax.sharding import PartitionSpec as P

F32 = jnp.float32
BF16 = jnp.bfloat16
D = 256
COLS = 128
OWN = 16
FRAME = OWN + 6
PADDED = 144
NEG = -1e30
KEYS = 160
LANES = 128
NT = (((1,), (1,)), ((), ()))
TN = (((0,), (0,)), ((), ()))
VMEM_BYTES = 58 * 1024 * 1024

BUFFERS = {
    "halo": ((2, 3, COLS, D), BF16),
    "shifted": ((2, PADDED, D), F32),
    "normed": ((FRAME, COLS, D), BF16),
    "k_win": ((FRAME, 16, 16, D), BF16),
    "v_win": ((FRAME, 16, 16, D), BF16),
    "q_tiles": ((2, 16, 64, D), BF16),
    "g_tiles": ((2, 16, 64, D), BF16),
    "attended": ((OWN, COLS, D), BF16),
    "joined": ((FRAME, COLS, 3 * D), BF16),
    "bias": ((3, 3, KEYS, LANES), F32),
    "acc": ((FRAME, PADDED, 2 * D), F32),
    "gn": ((OWN, COLS, D), F32),
    "sums": ((32, 16, 512), BF16),
    "rim_out": ((2, 3, COLS, D), BF16),
    "rim_in": ((2, 3, COLS, D), BF16),
}


def dot(a, b, dims=(((1,), (0,)), ((), ()))):
    return lax.dot_general(a, b, dims, preferred_element_type=F32)


def inverse_rms(wide):
    return lax.rsqrt(jnp.mean(wide * wide, axis=-1, keepdims=True) + 1e-6)


def windows(b, x, slot, frame_row):
    wide = x.astype(F32)
    normed = wide * inverse_rms(wide) * b.gain[...]
    b.normed[frame_row] = normed.astype(BF16)
    b.shifted[slot, 4 : 4 + COLS, :] = normed
    rows = jnp.concatenate([b.shifted[slot, 8 * j : 8 * j + 16, :] for j in range(16)], axis=0)
    kv = dot(rows.astype(BF16), b.w_in[:, D:])
    b.k_win[frame_row] = kv[:, :D].astype(BF16).reshape(16, 16, D)
    b.v_win[frame_row] = kv[:, D:].astype(BF16).reshape(16, 16, D)


def clear(b):
    b.shifted[...] = jnp.zeros_like(b.shifted)
    for r in range(3):
        b.joined[r, :, :D] = jnp.zeros((COLS, D), BF16)
        b.joined[OWN + 3 + r, :, :D] = jnp.zeros((COLS, D), BF16)

    def zero_row(r, carry):
        b.acc[r] = jnp.zeros((PADDED, 2 * D), F32)
        return carry

    lax.fori_loop(0, FRAME, zero_row, 0)


def mask(b, here, last):
    key = lax.broadcasted_iota(jnp.int32, (KEYS, LANES), 0)
    lane = lax.broadcasted_iota(jnp.int32, (KEYS, LANES), 1)
    k_row, k_col = key // 16, key % 16
    q_row, q_col = (lane % 32) // 8, lane % 8
    near = (k_row - q_row >= 0) & (k_row - q_row <= 6) & (k_col - q_col >= 1) & (k_col - q_col <= 7)
    inside = (near & ((k_row >= 3) | (here > 0)), near, near & ((k_row < 7) | (here < last)))
    for rows in range(3):
        for side, ok in enumerate((k_col >= 4, k_col >= 0, k_col < 12)):
            b.bias[rows, side] = jnp.where(inside[rows] & ok, 0.0, NEG)


def own_rows(b):
    def tile_order(pair):
        return [
            jnp.concatenate([pair[8 * j : 8 * j + 8], pair[COLS + 8 * j : COLS + 8 * j + 8]], axis=0)
            for j in range(16)
        ]

    def own_pair(i, carry):
        first = 2 * i
        half = i // 4
        place = pl.multiple_of((i % 4) * 16, 16)
        windows(b, b.tok[first], 0, first + 3)
        windows(b, b.tok[first + 1], 1, first + 4)
        both = b.normed[pl.ds(first + 3, 2)].reshape(2 * COLS, D)
        q = dot(both, b.w_in[:, :D])
        for j, tile in enumerate(tile_order(q)):
            b.q_tiles[half, j, pl.ds(place, 16), :] = (tile.astype(BF16).astype(F32) * 0.125).astype(BF16)
        g = dot(b.cot[pl.ds(first, 2)].reshape(2 * COLS, D), b.w_out[...], NT)
        for j, tile in enumerate(tile_order(g)):
            b.g_tiles[half, j, pl.ds(place, 16), :] = tile.astype(BF16)
        return carry

    lax.fori_loop(0, 8, own_pair, 0)


def halo_rows(b):
    def halo_row(r, carry):
        windows(b, b.halo[0, r], 0, r)
        windows(b, b.halo[1, r], 1, OWN + 3 + r)
        return carry

    for r in range(3):
        halo_row(r, 0)


def attend(b):
    head_lane = lax.broadcasted_iota(jnp.int32, (32, D), 1) // 64

    def by_head(source, tile):
        band, j, side = tile
        rows = source[band // 2, j, 32 * (band % 2) : 32 * (band % 2) + 32]
        return jnp.concatenate(
            [jnp.where(head_lane == h, rows, jnp.zeros_like(rows)) for h in range(4)], axis=0
        )

    def of_heads(full):
        out = full[96:128]
        for h in (2, 1, 0):
            out = jnp.where(head_lane == h, full[32 * h : 32 * h + 32], out)
        return out.reshape(4, 8, D)

    def add(tile, lanes, term):
        band, j, side = tile
        b.acc[4 * band : 4 * band + 10, pl.ds(pl.multiple_of(8 * j, 8), 16), lanes] += term.reshape(10, 16, D)

    def some_tiles(tiles):
        n = range(len(tiles))
        k = [b.k_win[4 * band : 4 * band + 10, j].reshape(KEYS, D) for band, j, side in tiles]
        v = [b.v_win[4 * band : 4 * band + 10, j].reshape(KEYS, D) for band, j, side in tiles]
        q = [by_head(b.q_tiles, tile) for tile in tiles]
        g = [by_head(b.g_tiles, tile) for tile in tiles]
        s = [dot(k[i], q[i], NT) + b.bias[(0, 1, 1, 2)[u[0]], u[2]] for i, u in enumerate(tiles)]
        dp = [dot(v[i], g[i], NT) for i in n]
        e = [jnp.exp(s[i] - jnp.max(s[i], axis=0, keepdims=True)) for i in n]
        p = [e[i] * (1.0 / jnp.sum(e[i], axis=0, keepdims=True)) for i in n]
        weights = [p[i].astype(BF16) for i in n]
        delta = [jnp.sum(p[i] * dp[i], axis=0, keepdims=True) for i in n]
        ds = [(p[i] * (dp[i] - delta[i])).astype(BF16) for i in n]
        att = [of_heads(dot(weights[i], v[i], TN)) for i in n]
        dq = [of_heads(dot(ds[i], k[i], TN)) * 0.125 for i in n]
        for i, u in enumerate(tiles):
            add(u, slice(D, 2 * D), dot(weights[i], g[i]))
        for i, u in enumerate(tiles):
            add(u, slice(0, D), dot(ds[i], q[i]))
        for i in range(0, len(tiles), 2):
            band, j, side = tiles[i]
            cols = pl.ds(pl.multiple_of(8 * j, 16), 16)
            b.attended[4 * band : 4 * band + 4, cols, :] = jnp.concatenate(att[i : i + 2], axis=1).astype(BF16)
            b.joined[4 * band + 3 : 4 * band + 7, cols, :D] = jnp.concatenate(dq[i : i + 2], axis=1).astype(BF16)

    def columns(jp, carry):
        sides = jnp.where(jp == 0, 0, 1), jnp.where(jp == 7, 2, 1)
        tiles = [(band, 2 * jp + i, sides[i]) for band in range(4) for i in range(2)]
        some_tiles(tiles)
        return carry

    lax.fori_loop(0, 8, columns, 0, unroll=4)


def round_keys(b):
    def key_row(r, carry):
        b.joined[r, :, D:] = b.acc[r, 4 : 4 + COLS, :].astype(BF16)
        return carry

    lax.fori_loop(0, FRAME, key_row, 0, unroll=True)


def weight_sums(b, part):
    lanes = pl.ds(pl.multiple_of(128 * part, 128), 128)
    g_in = dot(b.normed[:, :, lanes].reshape(FRAME * COLS, 128), b.joined[...].reshape(FRAME * COLS, 3 * D), TN)
    g_out = dot(b.attended[:, :, lanes].reshape(OWN * COLS, 128), b.cot[...].reshape(OWN * COLS, D), TN)
    for g in range(8):
        span = slice(16 * g, 16 * g + 16)
        b.sums[16 * part + 2 * g] = g_in[span, :512].astype(BF16)
        b.sums[16 * part + 2 * g + 1] = jnp.concatenate([g_in[span, 512:], g_out[span]], axis=1).astype(BF16)


def rim_rows(b):
    for side, first in ((0, 0), (1, OWN + 3)):
        rows = b.joined[first : first + 3].reshape(3 * COLS, 3 * D)
        b.rim_out[side] = dot(rows, b.w_in[...], NT).reshape(3, COLS, D).astype(BF16)


def own_gn(b):
    def four(i, carry):
        rows = b.joined[pl.ds(3 + 4 * i, 4)].reshape(4 * COLS, 3 * D)
        b.gn[pl.ds(4 * i, 4)] = dot(rows, b.w_in[...], NT).reshape(4, COLS, D)
        return carry

    lax.fori_loop(0, 4, four, 0)


def finish(b, row, rim=None):
    wide = b.tok[row].astype(F32)
    inv = inverse_rms(wide)
    gn = b.gn[row]
    if rim is not None:
        gn = gn + rim.astype(F32)
    gained = gn * b.gain[...]
    mean = jnp.mean(gained * wide, axis=-1, keepdims=True)
    b.gt[row] = (inv * (gained - wide * (inv * inv * mean))).astype(BF16)


def finish_rows(b, low, high):
    def body(r, carry):
        finish(b, r)
        return carry

    lax.fori_loop(low, high, body, 0)


def block_kernel(names, *refs):
    b = SimpleNamespace(**dict(zip(names, refs)))
    rows = lax.axis_index("rows")
    count = lax.axis_size("rows")
    x = lax.axis_index("dp")
    core = rows % 2
    z = (rows // 2) % 8
    y = rows // 16
    me = y * 4 + x
    before = {"rows": (rows + count - 1) % count, "dp": x}
    after = {"rows": (rows + 1) % count, "dp": x}
    partner = {"rows": rows + 1 - 2 * core, "dp": x}
    mine = 16 * core
    other = 16 - mine

    def away(i):
        return i + i // 2 - 2 * (i // 3)

    def offsets(i):
        n = (16 - i) % 16
        return away(n // 4), away(n % 4)

    def in_plane(i):
        by_y, by_x = offsets(i)
        to_y, to_x = (y + by_y) % 4, (x + by_x) % 4
        return {"rows": (to_y * 8 + z) * 2 + core, "dp": to_x}, to_y * 4 + to_x

    def from_plane(i):
        by_y, by_x = offsets(i)
        return ((y + 4 - by_y) % 4) * 4 + (x + 4 - by_x) % 4

    def along_z(i):
        by_z = 4 + (i // 2) * (2 * (i % 2) - 1)
        return {"rows": (y * 8 + (z + by_z) % 8) * 2 + core, "dp": x}

    def remote(src, dst, send, recv, where):
        return pltpu.make_async_remote_copy(
            src_ref=src, dst_ref=dst, send_sem=send, recv_sem=recv,
            device_id=where, device_id_type=pl.DeviceIdType.MESH,
        )

    loads = [
        pltpu.make_async_copy(src, dst, b.load.at[i])
        for i, (src, dst) in enumerate(
            ((b.tok_hbm, b.tok), (b.w_in_hbm, b.w_in), (b.gain_hbm, b.gain), (b.w_out_hbm, b.w_out), (b.cot_hbm, b.cot))
        )
    ]
    for copy in loads:
        copy.start()
    barrier = pltpu.get_barrier_semaphore()

    def greet(where):
        pl.semaphore_signal(barrier, inc=1, device_id=where, device_id_type=pl.DeviceIdType.MESH)

    def greet_plane(i, carry):
        greet(in_plane(i)[0])
        return carry

    def greet_z(i, carry):
        greet(along_z(i))
        return carry

    greet(before)
    greet(after)
    greet(partner)
    lax.fori_loop(1, 16, greet_plane, 0)
    lax.fori_loop(1, 8, greet_z, 0)
    pl.semaphore_wait(barrier, 25)

    def halo_copies():
        return (
            remote(b.tok_hbm.at[pl.ds(OWN - 3, 3)], b.halo.at[0], b.near_send.at[0], b.near_recv.at[0], after),
            remote(b.tok_hbm.at[pl.ds(0, 3)], b.halo.at[1], b.near_send.at[1], b.near_recv.at[1], before),
        )

    def rim_copies():
        return (
            remote(b.rim_out.at[0], b.rim_in.at[1], b.near_send.at[2], b.near_recv.at[2], before),
            remote(b.rim_out.at[1], b.rim_in.at[0], b.near_send.at[3], b.near_recv.at[3], after),
        )

    def core_scatter(i):
        place = in_plane(i)[1]
        return remote(b.sums.at[other + place], b.core_got.at[i], b.core_send.at[i], b.core_recv.at[i], partner)

    def scatter(i):
        where, place = in_plane(i)
        return remote(b.paired.at[i], b.plane_got.at[i], b.plane_send.at[i], b.plane_recv.at[i], where)

    def z_share(i):
        where = along_z(i)
        return remote(b.z_all.at[z], b.z_all.at[z], b.z_send.at[i], b.z_recv.at[i], where)

    def gather(i):
        where, place = in_plane(i)
        return remote(b.full.at[mine + me], b.full.at[mine + me], b.out_send.at[i], b.out_recv.at[i], where)

    def core_gather(i):
        chunk = b.full.at[mine + from_plane(i)]
        return remote(chunk, chunk, b.last_send.at[i], b.last_recv.at[i], partner)

    def each(make, low, high, act):
        def body(i, carry):
            act(make(i))
            return carry

        lax.fori_loop(low, high, body, 0)

    def start(copy):
        copy.start()

    def wait_send(copy):
        copy.wait_send()

    def wait_recv(copy):
        copy.wait_recv()

    for copy in halo_copies():
        copy.start()
    clear(b)
    mask(b, rows, count - 1)
    for copy in loads:
        copy.wait()
    own_rows(b)
    for copy in halo_copies():
        copy.wait_recv()
    halo_rows(b)
    attend(b)
    round_keys(b)
    weight_sums(b, 1 - core)
    stores = [
        pltpu.make_async_copy(b.gt.at[pl.ds(low, n)], b.gt_hbm.at[pl.ds(low, n)], b.store.at[i])
        for i, (low, n) in enumerate(((3, 10), (0, 3), (OWN - 3, 3)))
    ]
    each(core_scatter, 1, 16, start)
    core_scatter(0).start()
    weight_sums(b, core)
    rim_rows(b)
    for copy in rim_copies():
        copy.start()

    def pair(i):
        core_scatter(i).wait_recv()
        return b.sums[mine + in_plane(i)[1]].astype(F32) + b.core_got[i].astype(F32)

    def pair_and_send(i, carry):
        b.paired[i] = pair(i).astype(BF16)
        scatter(i).start()
        return carry

    lax.fori_loop(1, 16, pair_and_send, 0)
    own_gn(b)

    def add_plane(i, total):
        scatter(i).wait_recv()
        return total + b.plane_got[i].astype(F32)

    total = lax.fori_loop(1, 16, add_plane, pair(0))
    b.z_all[z] = total.astype(BF16)
    each(z_share, 1, 8, start)
    finish_rows(b, 3, 13)
    stores[0].start()
    each(z_share, 1, 8, wait_recv)
    whole = b.z_all[0].astype(F32)
    for i in range(1, 8):
        whole = whole + b.z_all[i].astype(F32)
    b.full[mine + me] = whole.astype(BF16)
    each(gather, 1, 16, start)
    core_gather(0).start()
    for copy in rim_copies():
        copy.wait_recv()

    def edge(r, carry):
        finish(b, r, b.rim_in[0, r])
        finish(b, OWN - 3 + r, b.rim_in[1, r])
        return carry

    lax.fori_loop(0, 3, edge, 0)
    stores[1].start()
    stores[2].start()
    for copy in halo_copies() + rim_copies():
        copy.wait_send()
    each(core_scatter, 0, 16, wait_send)
    each(scatter, 1, 16, wait_send)
    each(z_share, 1, 8, wait_send)

    def pass_on(i, carry):
        gather(16 - i).wait_recv()
        core_gather(16 - i).start()
        return carry

    lax.fori_loop(1, 16, pass_on, 0)
    each(core_gather, 0, 16, wait_recv)
    for copy in stores:
        copy.wait()
    each(gather, 1, 16, wait_send)
    each(core_gather, 0, 16, wait_send)


def block(tok, cot, gain, w_in, w_out):
    vmem, hbm = pl.BlockSpec(memory_space=pltpu.VMEM), pl.BlockSpec(memory_space=pltpu.HBM)
    dma = pltpu.SemaphoreType.DMA
    outs = {"gt_hbm": ((OWN, COLS, D), BF16), "full": ((32, 16, 512), BF16)}
    slots = {
        "tok": ((OWN, COLS, D), BF16),
        "cot": ((OWN, COLS, D), BF16),
        "gain": ((1, D), F32),
        "w_in": ((D, 3 * D), BF16),
        "w_out": ((D, D), BF16),
        "gt": ((OWN, COLS, D), BF16),
        "core_got": ((16, 16, 512), BF16),
        "paired": ((16, 16, 512), BF16),
        "plane_got": ((16, 16, 512), BF16),
        "z_all": ((8, 16, 512), BF16),
    }
    sems = {
        "load": 5, "store": 3, "near_send": 4, "near_recv": 4, "core_send": 16, "core_recv": 16, "plane_send": 16, "plane_recv": 16,
        "z_send": 8, "z_recv": 8, "out_send": 16, "out_recv": 16,
        "last_send": 16, "last_recv": 16,
    }
    names = ["tok_hbm", "cot_hbm", "gain_hbm", "w_in_hbm", "w_out_hbm", *outs, *BUFFERS, *slots, *sems]

    def kernel(*refs):
        block_kernel(names, *refs)

    return pl.pallas_call(
        kernel,
        out_shape=tuple(jax.ShapeDtypeStruct(*o) for o in outs.values()),
        in_specs=[hbm] * 5,
        out_specs=(hbm, vmem),
        scratch_shapes=[
            *(pltpu.VMEM(*s) for s in BUFFERS.values()),
            *(pltpu.VMEM(*s) for s in slots.values()),
            *(dma((n,)) for n in sems.values()),
        ],
        compiler_params=pltpu.CompilerParams(
            collective_id=0, has_side_effects=True, vmem_limit_bytes=VMEM_BYTES
        ),
    )(tok, cot, gain, w_in, w_out)


def outputs(gt, full, gain, w_in, factor):
    def kernel(gt_hbm, full_hbm, gain_hbm, w_hbm, gt_out, g_in_out, g_out_out, g_gain_out,
               rows, full_ref, gain_ref, w, g_in, g_out, g_gain, sem):
        quarters = [pl.ds(4 * i, 4) for i in range(4)]
        spans = [pl.ds(64 * i, 64) for i in range(4)]

        def copies(first, pairs):
            return [pltpu.make_async_copy(src, dst, sem.at[first + i]) for i, (src, dst) in enumerate(pairs)]

        parts = copies(0, [(full_hbm.at[pl.ds(8 * i, 8)], full_ref.at[pl.ds(8 * i, 8)]) for i in range(4)])
        small = copies(4, [(w_hbm, w), (gain_hbm, gain_ref)])
        reads = copies(6, [(gt_hbm.at[r], rows.at[r]) for r in quarters])
        writes = copies(10, [(rows.at[r], gt_out.at[r]) for r in quarters])
        in_writes = copies(14, [(g_in.at[r], g_in_out.at[r]) for r in spans])
        out_writes = copies(18, [(g_out.at[r], g_out_out.at[r]) for r in spans])
        gain_write = pltpu.make_async_copy(g_gain, g_gain_out, sem.at[22])
        for copy in parts + small + reads:
            copy.start()
        per_row = []
        for i in range(4):
            parts[i].wait()
            for g in range(4 * i, 4 * i + 4):
                span = slice(16 * g, 16 * g + 16)
                right = full_ref[2 * g + 1].astype(F32) * factor
                g_in[span, :512] = full_ref[2 * g].astype(F32) * factor
                g_in[span, 512:] = right[:, :256]
                g_out[span, :] = right[:, 256:]
            in_writes[i].start()
            out_writes[i].start()
            reads[i].wait()
            writes[i].start()
            if i == 0:
                for copy in small:
                    copy.wait()
            rows_here = slice(64 * i, 64 * i + 64)
            term = g_in[rows_here, :] * w[rows_here, :].astype(F32)
            per_row.append(jnp.sum(term, axis=1, keepdims=True))
        column = jnp.broadcast_to(jnp.concatenate(per_row, axis=0), (D, 128))
        g_gain[...] = jnp.transpose(column)[0:1] / gain_ref[...]
        gain_write.start()
        for copy in writes + in_writes + out_writes + [gain_write]:
            copy.wait()

    hbm = pl.BlockSpec(memory_space=pltpu.HBM)
    return pl.pallas_call(
        kernel,
        out_shape=(
            jax.ShapeDtypeStruct((OWN, COLS, D), BF16),
            jax.ShapeDtypeStruct((D, 3 * D), F32),
            jax.ShapeDtypeStruct((D, D), F32),
            jax.ShapeDtypeStruct((1, D), F32),
        ),
        in_specs=[hbm] * 4,
        out_specs=(hbm,) * 4,
        scratch_shapes=[
            pltpu.VMEM((OWN, COLS, D), BF16),
            pltpu.VMEM((32, 16, 512), BF16),
            pltpu.VMEM((1, D), F32),
            pltpu.VMEM((D, 3 * D), BF16),
            pltpu.VMEM((D, 3 * D), F32),
            pltpu.VMEM((D, D), F32),
            pltpu.VMEM((1, D), F32),
            pltpu.SemaphoreType.DMA((23,)),
        ],
        compiler_params=pltpu.CompilerParams(vmem_limit_bytes=VMEM_BYTES),
    )(gt, full, gain, w_in)


def local(tokens, norm_gain, in_weight, out_weight, cotangent):
    factor = 1.0 / math.sqrt(lax.axis_size("rows") * lax.axis_size("dp") * OWN * COLS)
    gain = norm_gain.reshape(1, D)
    gt, full = block(tokens[0], cotangent[0], gain, in_weight, out_weight)
    gt, g_in, g_out, g_gain = outputs(gt, full, gain, in_weight, factor)
    return gt[None], g_in, g_out, g_gain.reshape(D)


def solution(mesh):
    return jax.shard_map(
        local,
        mesh=mesh,
        in_specs=(P("dp", "rows", None, None), P(), P(), P(), P("dp", "rows", None, None)),
        out_specs=(P("dp", "rows", None, None), P(), P(), P()),
        check_vma=False,
    )
```
